256 devices in a mesh: seg: 64 (over x, z, core), head: 4 (over y).
Axes of the slice: x: 4, y: 4, z: 8, core: 2. Of those that a mesh axis runs over, the one named last changes fastest.
Arguments:
- tokens: bfloat16 [65536, 1024], P('seg'), may hold values from -50 to 50
- norm_gain: bfloat16 [1024], replicated, may hold values from 0.099609375 to 1.8984375
- qkv_weight: bfloat16 [3, 1024, 1024], P(None, None, 'head'), may hold values from -1.5 to 1.5
- out_weight: bfloat16 [1024, 1024], replicated, may hold values from -0.1875 to 0.1875
- offsets: int32 [16, 2], P('head'), may hold values from 0 to 31, as said below
Outputs:
- projected: bfloat16 [65536, 1024], P('seg', 'head')
The draws below stay inside these ranges and needn't reach their ends.
Inputs may be any that keep to these rules, and one draw needn't show every extreme that they name: offsets[h, 0] is below 4 and offsets[h, 1] below 32.
All inputs are finite; a program needn't handle non-finite values.
Results may differ from the reference program's by a relative error of at most 0.012.
The reference program's roundings to bfloat16 on the way count: a program that leaves them out, or rounds other values in their place, can miss the bound.
Values may be sent and summed in bfloat16 or wider, within the bound.
No kernel may reach another device: no remote copies, remote signals or barrier semaphores. Data moves between devices by JAX's collectives and lax.ppermute only.
A program may use at most 128 MiB of HBM per device.

```python
import math
import jax
import jax.numpy as jnp
from jax import lax

D = 1024
HEADS = 16
HEAD_DIM = 64
MID_RATE = 4
GROUP = 2048
FAR_RATE = 32
TOKENS = 65536


def draw_tokens(key, part):
    key = jax.random.fold_in(key, 11)
    baseline = jax.random.normal(key, (TOKENS, D), jnp.float32)
    return jnp.clip(baseline, -6.0, 6.0).astype(jnp.bfloat16)


def draw_qkv_weight(key, part):
    key = jax.random.fold_in(key, 23)
    spread = 2.0 / math.sqrt(D)
    own = jax.random.normal(key, (3, D, D), jnp.float32) * spread
    return jnp.clip(own, -1.5, 1.5).astype(jnp.bfloat16)


def draw_offsets(key, part):
    key = jax.random.fold_in(key, 37)
    middle = jax.random.randint(jax.random.fold_in(key, 1), (HEADS,), 0, MID_RATE)
    distant = jax.random.randint(jax.random.fold_in(key, 2), (HEADS,), 0, FAR_RATE)
    shuffled = jax.random.permutation(jax.random.fold_in(key, 3), HEADS)
    distant = distant.at[shuffled[0]].set(FAR_RATE - 1).at[shuffled[1]].set(0)
    middle = middle.at[shuffled[2]].set(MID_RATE - 1).at[shuffled[3]].set(0)
    return jnp.stack([middle, distant], axis=1).astype(jnp.int32)


def scatter_about(key, extent, scale, reach, held_as=jnp.bfloat16):
    return jnp.clip(scale * jax.random.normal(key, extent, jnp.float32), -reach, reach).astype(held_as)


def setup_inputs(seed: int = 0) -> dict:
    arg_keys = jax.random.split(jax.random.key(seed), 6)
    return {
        "tokens": draw_tokens(jax.random.fold_in(arg_keys[5], 71), 0),
        "norm_gain": jnp.clip(1.0 + 0.18 * jax.random.normal(arg_keys[1], (D,), jnp.float32), 0.099609375, 1.8984375).astype(jnp.bfloat16),
        "qkv_weight": draw_qkv_weight(jax.random.fold_in(arg_keys[5], 71), 0),
        "out_weight": scatter_about(arg_keys[3], (D, D), D ** -0.5, 0.1875),
        "offsets": draw_offsets(jax.random.fold_in(arg_keys[5], 71), 0),
    }


EPS = 1e-06
NEG = -1e+30

def attend_head(queries, key_rows, value_rows):
    scores = jnp.dot(queries, key_rows.T, preferred_element_type=jnp.float32) * HEAD_DIM ** (-0.5)
    row_peak = lax.optimization_barrier(jnp.max(scores, axis=1, keepdims=True))
    weights = jnp.exp(scores - row_peak)
    row_total = lax.optimization_barrier(jnp.sum(weights, axis=1, keepdims=True))
    blended = jnp.dot(weights.astype(jnp.bfloat16), value_rows, preferred_element_type=jnp.float32) / row_total
    return (blended, row_peak[:, 0] + jnp.log(row_total[:, 0]))

def segment_items(items):
    return attend_head(items[0], items[1], items[2])

def branch(queries, key_rows, value_rows, dilation, offset):
    span = GROUP * dilation

    def select(values_in):
        grouped = values_in.reshape(TOKENS // span, GROUP, dilation, HEAD_DIM)
        return lax.dynamic_index_in_dim(grouped, offset, axis=2, keepdims=False)
    blended, log_total = lax.map(segment_items, (select(queries), select(key_rows), select(value_rows)))
    chosen = jnp.arange(dilation, dtype=jnp.int32) == offset
    full = jnp.where(chosen[None, None, :, None], blended[:, :, None, :], 0.0).reshape(TOKENS, HEAD_DIM)
    full_log = jnp.where(chosen[None, None, :], log_total[:, :, None], NEG).reshape(TOKENS)
    return (full, full_log)

def head_work(items):
    queries, key_rows, value_rows, offset_pair = items
    near_out, near_log = branch(queries, key_rows, value_rows, 1, jnp.zeros((), jnp.int32))
    middle_out, middle_log = branch(queries, key_rows, value_rows, MID_RATE, offset_pair[0])
    far_out, far_log = branch(queries, key_rows, value_rows, FAR_RATE, offset_pair[1])
    row_peak = jnp.maximum(jnp.maximum(near_log, middle_log), far_log)
    near_weight = jnp.exp(near_log - row_peak)[:, None]
    middle_weight = jnp.exp(middle_log - row_peak)[:, None]
    far_weight = jnp.exp(far_log - row_peak)[:, None]
    return (near_weight * near_out + middle_weight * middle_out + far_weight * far_out) / (near_weight + middle_weight + far_weight)

def reference(tokens, norm_gain, qkv_weight, out_weight, offsets):
    widened = tokens.astype(jnp.float32)
    mean_square = lax.optimization_barrier(jnp.mean(widened * widened, axis=1, keepdims=True))
    normed = (widened * lax.rsqrt(mean_square + EPS) * norm_gain.astype(jnp.float32)).astype(jnp.bfloat16)
    queries = jnp.dot(normed, qkv_weight[0], preferred_element_type=jnp.float32).astype(jnp.bfloat16)
    key_rows = jnp.dot(normed, qkv_weight[1], preferred_element_type=jnp.float32).astype(jnp.bfloat16)
    value_rows = jnp.dot(normed, qkv_weight[2], preferred_element_type=jnp.float32).astype(jnp.bfloat16)
    queries = jnp.transpose(queries.reshape(TOKENS, HEADS, HEAD_DIM), (1, 0, 2))
    key_rows = jnp.transpose(key_rows.reshape(TOKENS, HEADS, HEAD_DIM), (1, 0, 2))
    value_rows = jnp.transpose(value_rows.reshape(TOKENS, HEADS, HEAD_DIM), (1, 0, 2))
    per_head = lax.map(head_work, (queries, key_rows, value_rows, offsets.astype(jnp.int32)))
    attention = jnp.transpose(per_head, (1, 0, 2)).reshape(TOKENS, D).astype(jnp.bfloat16)
    return jnp.dot(attention, out_weight, preferred_element_type=jnp.float32).astype(jnp.bfloat16)
```

```python
import functools

import jax
import jax.numpy as jnp
from jax import lax
from jax.experimental import pallas as pl
from jax.experimental.pallas import tpu as pltpu
from jax.sharding import PartitionSpec as P

HEAD_DIM = 64
MID_RATE = 4
FAR_RATE = 32
EPS = 1e-06
LANES = 128
BF = jnp.bfloat16
F32 = jnp.float32
SCALE = 1.4426950408889634 * HEAD_DIM ** (-0.5)
VMEM = pl.BlockSpec(memory_space=pltpu.VMEM)
SMEM = pl.BlockSpec(memory_space=pltpu.SMEM)
PARAMS = pltpu.CompilerParams(vmem_limit_bytes=56 * 2**20)


def shape(rows, columns, dtype=BF):
    return jax.ShapeDtypeStruct((rows, columns), dtype)


def left_lanes():
    return lax.broadcasted_iota(jnp.int32, (1, LANES), 1) < HEAD_DIM


def project_kernel(
    offsets, tokens, gain, weight, q_out, kv0_out, kv1_out, qm_out, kvm_out, qf_out, kvf_out, held
):
    rows = tokens.shape[0]
    x = tokens[...].astype(F32)
    mean_square = jnp.mean(x * x, axis=1, keepdims=True)
    normed = (x * lax.rsqrt(mean_square + EPS) * gain[...].astype(F32)).astype(BF)
    near = (kv0_out, kv1_out)
    for part in range(3):
        y = jnp.dot(normed, weight[part], preferred_element_type=F32)
        yb = y.astype(BF)
        for pair in range(2):
            held[2 * part + pair] = y[:, pair * LANES : (pair + 1) * LANES]
        if part == 0:
            q_out[...] = yb
        else:
            for pair in range(2):
                near[pair][:, (part - 1) * LANES : part * LANES] = yb[
                    :, pair * LANES : (pair + 1) * LANES
                ]
    left = left_lanes()
    for rate, which, q_to, kv_to in ((MID_RATE, 0, qm_out, kvm_out), (FAR_RATE, 1, qf_out, kvf_out)):
        count = rows // rate
        for pair in range(2):
            o0 = offsets[2 * pair, which]
            o1 = offsets[2 * pair + 1, which]
            for part in range(3):
                source = held.at[2 * part + pair]
                a = source[pl.ds(o0, count, stride=rate), :]
                b = source[pl.ds(o1, count, stride=rate), :]
                picked = jnp.where(left, a, b).astype(BF)
                if part == 0:
                    q_to[:, pair * LANES : (pair + 1) * LANES] = picked
                else:
                    c = (2 * pair + part - 1) * LANES
                    kv_to[:, c : c + LANES] = picked


def project(offsets, tokens, gain, weight):
    rows, width = tokens.shape
    own = weight.shape[2]
    block = 512

    def rowed(count, columns):
        return pl.BlockSpec((count, columns), lambda i: (i, 0))

    mid, far = block // MID_RATE, block // FAR_RATE
    return pl.pallas_call(
        project_kernel,
        grid=(rows // block,),
        out_shape=[
            shape(rows, own),
            shape(rows, own),
            shape(rows, own),
            shape(rows // MID_RATE, own),
            shape(rows // MID_RATE, 2 * own),
            shape(rows // FAR_RATE, own),
            shape(rows // FAR_RATE, 2 * own),
        ],
        in_specs=[
            SMEM,
            rowed(block, width),
            pl.BlockSpec((1, width), lambda i: (0, 0)),
            pl.BlockSpec((3, width, own), lambda i: (0, 0, 0)),
        ],
        out_specs=[
            rowed(block, own),
            rowed(block, own),
            rowed(block, own),
            rowed(mid, own),
            rowed(mid, 2 * own),
            rowed(far, own),
            rowed(far, 2 * own),
        ],
        scratch_shapes=[pltpu.VMEM((6, block, LANES), F32)],
        compiler_params=PARAMS,
    )(offsets, tokens, gain.reshape(1, width), weight)


def fill(keys, values, at, key_rows, value_rows):
    left = left_lanes()
    count = key_rows.shape[0]
    one = jnp.ones_like(value_rows)
    keys[:, at : at + count] = jnp.concatenate([key_rows, key_rows], axis=1).T
    values[0, at : at + count, :] = jnp.where(left, value_rows, one)
    values[1, at : at + count, :] = jnp.where(left, one, value_rows)


def attend(q, head, keys, values):
    left = left_lanes()
    scaled = q.astype(F32) * SCALE
    scaled = jnp.where(left, scaled, 0.0) if head == 0 else jnp.where(left, 0.0, scaled)
    high = scaled.astype(BF)
    low = (scaled - high.astype(F32)).astype(BF)
    scores = jnp.dot(jnp.concatenate([high, low], axis=1), keys[...], preferred_element_type=F32)
    peak = jnp.max(scores, axis=1, keepdims=True)
    weights = jnp.exp2(scores - peak).astype(BF)
    return jnp.dot(weights, values[head], preferred_element_type=F32), peak


def near_kernel(q, own, theirs, acc_out, peak_out, keys, values):
    rows = q.shape[0]
    block = 256
    for i, kv in enumerate((own, theirs)):
        fill(keys, values, i * rows, kv[:, :LANES], kv[:, LANES:])

    def step(r, _):
        at = pl.ds(pl.multiple_of(r * block, block), block)
        for head in range(2):
            acc, peak = attend(q[at, :], head, keys, values)
            acc_out[head, at, :] = acc
            peak_out[head, at, :] = jnp.broadcast_to(peak, (block, LANES))
        return 0

    lax.fori_loop(0, rows // block, step, 0)


def near_attention(q, pair, own, theirs):
    rows = q.shape[0]
    return pl.pallas_call(
        near_kernel,
        grid=(1,),
        out_shape=[jax.ShapeDtypeStruct((2, rows, LANES), F32)] * 2,
        in_specs=[
            pl.BlockSpec((rows, LANES), lambda i: (0, pair)),
            pl.BlockSpec((rows, 2 * LANES), lambda i: (0, 0)),
            pl.BlockSpec((rows, 2 * LANES), lambda i: (0, 0)),
        ],
        out_specs=[pl.BlockSpec((2, rows, LANES), lambda i: (0, 0, 0))] * 2,
        scratch_shapes=[
            pltpu.VMEM((2 * LANES, 2 * rows), BF),
            pltpu.VMEM((2, 2 * rows, LANES), BF),
        ],
        compiler_params=PARAMS,
        cost_estimate=pl.CostEstimate(flops=8 * 10**9, bytes_accessed=4 * 10**6, transcendentals=0),
    )(q, own, theirs)


def merge_kernel(offsets, qm, qf, *refs):
    mids, fars = refs[0:8], refs[8:16]
    accs_in, peaks_in = refs[16:18], refs[18:20]
    out = refs[20]
    keys, values, acc, peak = refs[21:25]
    left = left_lanes()
    rows = out.shape[0]
    for pair in range(2):
        acc[...] = accs_in[pair][...]
        peak[...] = peaks_in[pair][...]
        lanes = slice(pair * LANES, (pair + 1) * LANES)
        k_at = slice(2 * pair * LANES, (2 * pair + 1) * LANES)
        v_at = slice((2 * pair + 1) * LANES, (2 * pair + 2) * LANES)
        for pieces, q, rate, which in ((mids, qm, MID_RATE, 0), (fars, qf, FAR_RATE, 1)):
            at = 0
            for piece in pieces:
                fill(keys, values, at, piece[:, k_at], piece[:, v_at])
                at += piece.shape[0]
            for head in range(2):
                more, more_peak = attend(q[:, lanes], head, keys, values)
                chosen = pl.ds(offsets[2 * pair + head, which], rows // rate, stride=rate)
                old, old_peak = acc.at[head][chosen, :], peak.at[head][chosen, :]
                top = jnp.maximum(old_peak, more_peak)
                acc.at[head][chosen, :] = old * jnp.exp2(old_peak - top) + more * jnp.exp2(
                    more_peak - top
                )
                peak.at[head][chosen, :] = top
        a, b = acc[0], acc[1]
        total = pltpu.roll(jnp.where(left, b, a), HEAD_DIM, 1)
        out[:, lanes] = (jnp.where(left, a, b) / total).astype(BF)


def merge(offsets, qm, qf, mids, fars, accs, peaks, rows):
    own = qm.shape[1]
    return pl.pallas_call(
        merge_kernel,
        out_shape=shape(rows, own),
        in_specs=[SMEM] + [VMEM] * (2 + 16 + 4),
        out_specs=VMEM,
        scratch_shapes=[
            pltpu.VMEM((2 * LANES, 2048), BF),
            pltpu.VMEM((2, 2048, LANES), BF),
            pltpu.VMEM((2, rows, LANES), F32),
            pltpu.VMEM((2, rows, LANES), F32),
        ],
        compiler_params=PARAMS,
        cost_estimate=pl.CostEstimate(flops=5 * 10**9, bytes_accessed=9 * 10**6, transcendentals=0),
    )(offsets, qm, qf, *mids, *fars, *accs, *peaks)


def out_kernel(me, a0, a1, a2, a3, weight, out):
    total = None
    for d, part in enumerate((a0, a1, a2, a3)):
        depth = part.shape[1]
        at = pl.multiple_of((me[0] ^ d) * depth, depth)
        term = jnp.dot(part[...], weight[pl.ds(at, depth), :], preferred_element_type=F32)
        total = term if total is None else total + term
    out[...] = total.astype(BF)


def project_out(me, parts, weight):
    rows, own = parts[0].shape
    block = 512
    width = weight.shape[0]
    return pl.pallas_call(
        out_kernel,
        out_shape=shape(rows, own),
        grid_spec=pltpu.PrefetchScalarGridSpec(
            num_scalar_prefetch=1,
            grid=(rows // block,),
            in_specs=[pl.BlockSpec((block, own), lambda i, me: (i, 0))] * 4
            + [pl.BlockSpec((width, own), lambda i, me: (0, me[0]))],
            out_specs=pl.BlockSpec((block, own), lambda i, me: (i, 0)),
        ),
        compiler_params=PARAMS,
    )(me, *parts, weight)


def seg_move(array, target):
    pairs = []
    for i in range(64):
        x, z, core = i // 16, i // 2 % 8, i % 2
        x, z, core = target(x, z, core)
        pairs.append((i, (x % 4 * 8 + z % 8) * 2 + core))
    return lax.ppermute(array, "seg", pairs)


def swap_core(array):
    return seg_move(array, lambda x, z, core: (x, z, 1 - core))


def near_z(array, distance):
    return seg_move(array, lambda x, z, core: (x, z ^ distance, core))


def both_ways(array, distance):
    return seg_move(array, lambda x, z, core: (x, z + (distance if core == 0 else -distance), core))


def along_x(array, distance):
    return seg_move(array, lambda x, z, core: (x ^ distance, z, core))


def shards(tokens, norm_gain, qkv_weight, out_weight, offsets):
    rows = tokens.shape[0]
    q, kv0, kv1, qm, kvm, qf, kvf = project(offsets, tokens, norm_gain, qkv_weight)
    other0, other1 = swap_core(kv0), swap_core(kv1)
    chip = jnp.concatenate([kvf, swap_core(kvf)], axis=0)
    line = jnp.concatenate(
        [kvf, both_ways(kvf, 4)] + [both_ways(chip, distance) for distance in (1, 2, 3)], axis=0
    )
    fars = [line] + [along_x(line, distance) for distance in (1, 2, 3)]
    fars = fars + [swap_core(piece) for piece in fars]
    mids = [kvm] + [near_z(kvm, distance) for distance in (1, 2, 3)]
    mids = mids + [swap_core(piece) for piece in mids]
    acc0, peak0 = near_attention(q, 0, kv0, other0)
    acc1, peak1 = near_attention(q, 1, kv1, other1)
    attention = merge(offsets, qm, qf, mids, fars, (acc0, acc1), (peak0, peak1), rows)
    me = lax.axis_index("head").astype(jnp.int32)
    parts = [attention] + [
        lax.ppermute(attention, "head", [(i, i ^ d) for i in range(4)]) for d in (1, 2, 3)
    ]
    return project_out(me.reshape(1), parts, out_weight)


def solution(mesh):
    placed = (P("seg", None), P(), P(None, None, "head"), P(), P("head", None))
    return jax.shard_map(
        shards, mesh=mesh, in_specs=placed, out_specs=P("seg", "head"), check_vma=False
    )
```

```python
import functools

import jax
import jax.numpy as jnp
from jax import lax
from jax.experimental import pallas as pl
from jax.experimental.pallas import tpu as pltpu
from jax.sharding import PartitionSpec as P

HEAD_DIM = 64
MID_RATE = 4
FAR_RATE = 32
GROUP = 2048
EPS = 1e-06
LANES = 128
BF = jnp.bfloat16
F32 = jnp.float32
SCALE = 1.4426950408889634 * HEAD_DIM ** (-0.5)
VMEM = pl.BlockSpec(memory_space=pltpu.VMEM)
SMEM = pl.BlockSpec(memory_space=pltpu.SMEM)
ANY = pl.BlockSpec(memory_space=pl.ANY)
PARAMS = pltpu.CompilerParams(vmem_limit_bytes=56 * 2**20)


def shape(*dims, dtype=BF):
    return jax.ShapeDtypeStruct(dims, dtype)


def left_lanes():
    return lax.broadcasted_iota(jnp.int32, (1, LANES), 1) < HEAD_DIM


def cost(flops, bytes_accessed):
    return pl.CostEstimate(flops=flops, bytes_accessed=bytes_accessed, transcendentals=0)


def project_kernel(
    offsets, tokens, gain, weight, q_out, kv0_out, kv1_out, qm_out, kvm_out, qf_out, kvf_out, held
):
    rows = tokens.shape[0]
    x = tokens[...].astype(F32)
    mean_square = jnp.mean(x * x, axis=1, keepdims=True)
    normed = (x * lax.rsqrt(mean_square + EPS) * gain[...].astype(F32)[None, :]).astype(BF)
    near = (kv0_out, kv1_out)
    for part in range(3):
        y = jnp.dot(normed, weight[part], preferred_element_type=F32)
        yb = y.astype(BF)
        for pair in range(2):
            held[2 * part + pair] = y[:, pair * LANES : (pair + 1) * LANES]
        if part == 0:
            q_out[...] = yb
        else:
            for pair in range(2):
                near[pair][:, (part - 1) * LANES : part * LANES] = yb[
                    :, pair * LANES : (pair + 1) * LANES
                ]
    left = left_lanes()
    for rate, which, q_to, kv_to in ((MID_RATE, 0, qm_out, kvm_out), (FAR_RATE, 1, qf_out, kvf_out)):
        count = rows // rate
        for pair in range(2):
            o0 = offsets[2 * pair, which]
            o1 = offsets[2 * pair + 1, which]
            for part in range(3):
                source = held.at[2 * part + pair]
                a = source[pl.ds(o0, count, stride=rate), :]
                b = source[pl.ds(o1, count, stride=rate), :]
                picked = jnp.where(left, a, b).astype(BF)
                if part == 0:
                    q_to[:, pair * LANES : (pair + 1) * LANES] = picked
                else:
                    c = (2 * pair + part - 1) * LANES
                    kv_to[:, c : c + LANES] = picked


def project(offsets, tokens, gain, weight):
    rows, width = tokens.shape
    own = weight.shape[2]
    block = 512

    def rowed(count, columns):
        return pl.BlockSpec((count, columns), lambda i: (i, 0))

    mid, far = block // MID_RATE, block // FAR_RATE
    return pl.pallas_call(
        project_kernel,
        grid=(rows // block,),
        out_shape=[
            shape(rows, own),
            shape(rows, own),
            shape(rows, own),
            shape(rows // MID_RATE, own),
            shape(rows // MID_RATE, 2 * own),
            shape(rows // FAR_RATE, own),
            shape(rows // FAR_RATE, 2 * own),
        ],
        in_specs=[
            SMEM,
            rowed(block, width),
            pl.BlockSpec((width,), lambda i: (0,)),
            pl.BlockSpec((3, width, own), lambda i: (0, 0, 0)),
        ],
        out_specs=[
            rowed(block, own),
            rowed(block, own),
            rowed(block, own),
            rowed(mid, own),
            rowed(mid, 2 * own),
            rowed(far, own),
            rowed(far, 2 * own),
        ],
        scratch_shapes=[pltpu.VMEM((6, block, LANES), F32)],
        compiler_params=PARAMS,
        cost_estimate=cost(2 * 10**9, 6 * 10**6),
    )(offsets, tokens, gain, weight)


def fill(keys, values, at, key_rows, value_rows):
    left = left_lanes()
    count = key_rows.shape[0]
    one = jnp.ones_like(value_rows)
    turned = key_rows.T
    for head in range(2):
        half = turned[head * HEAD_DIM : (head + 1) * HEAD_DIM]
        keys[head, :HEAD_DIM, at : at + count] = half
        keys[head, HEAD_DIM:, at : at + count] = half
    values[0, at : at + count, :] = jnp.where(left, value_rows, one)
    values[1, at : at + count, :] = jnp.where(left, one, value_rows)


def split_queries(q, head):
    left = left_lanes()
    scaled = q.astype(F32) * SCALE
    high = scaled.astype(BF).astype(F32)
    low = scaled - high
    if head == 0:
        both = jnp.where(left, high, pltpu.roll(low, HEAD_DIM, 1))
    else:
        both = jnp.where(left, pltpu.roll(high, HEAD_DIM, 1), low)
    return both.astype(BF)


def attend(jobs, slots):
    def scores(job):
        return jnp.dot(job[0](), job[1], preferred_element_type=F32)

    slots[0, : jobs[0][4]] = scores(jobs[0])
    for i, (_, _, values, done, count) in enumerate(jobs):
        if i + 1 < len(jobs):
            slots[(i + 1) % 2, : jobs[i + 1][4]] = scores(jobs[i + 1])
        s = slots[i % 2, :count]
        peak = jnp.max(s, axis=1, keepdims=True)
        weights = jnp.exp2(s - peak).astype(BF)
        done(jnp.dot(weights, values, preferred_element_type=F32), peak)


def near_kernel(q, own, theirs, _, acc_out, peak_out, keys, values, queries, slots):
    rows = q.shape[0]
    block = slots.shape[1]
    for i, kv in enumerate((own, theirs)):
        fill(keys, values, i * rows, kv[:, :LANES], kv[:, LANES:])
    jobs = []
    for head in range(2):
        queries[head] = split_queries(q[...], head)
        for r in range(rows // block):
            at = slice(r * block, (r + 1) * block)

            def done(acc, peak, head=head, at=at):
                acc_out[head, at, :] = acc
                peak_out[head, at, :] = jnp.broadcast_to(peak, acc.shape)

            jobs.append(
                (lambda head=head, at=at: queries[head, at, :], keys[head], values[head], done, block)
            )
    attend(jobs, slots)


def near_attention(q, pair, own, theirs, after):
    rows = q.shape[0]
    block = 256
    return pl.pallas_call(
        near_kernel,
        grid=(1,),
        out_shape=[shape(2, rows, LANES, dtype=F32)] * 2,
        in_specs=[
            pl.BlockSpec((rows, LANES), lambda i: (0, pair)),
            pl.BlockSpec((rows, 2 * LANES), lambda i: (0, 0)),
            pl.BlockSpec((rows, 2 * LANES), lambda i: (0, 0)),
            ANY,
        ],
        out_specs=[pl.BlockSpec((2, rows, LANES), lambda i: (0, 0, 0))] * 2,
        scratch_shapes=[
            pltpu.VMEM((2, LANES, GROUP), BF),
            pltpu.VMEM((2, GROUP, LANES), BF),
            pltpu.VMEM((2, rows, LANES), BF),
            pltpu.VMEM((2, block, GROUP), F32),
        ],
        compiler_params=PARAMS,
        cost_estimate=cost(8 * 10**9, 4 * 10**6),
    )(q, own, theirs, after)


def pair_columns(pair):
    return (
        slice(pair * LANES, (pair + 1) * LANES),
        slice(2 * pair * LANES, (2 * pair + 1) * LANES),
        slice((2 * pair + 1) * LANES, (2 * pair + 2) * LANES),
    )


def middle_kernel(q, *refs):
    pieces, (acc_out, peak_out, keys, values, slots) = refs[:8], refs[8:]
    count = q.shape[0]
    jobs = []
    for pair in range(2):
        lanes, k_at, v_at = pair_columns(pair)
        at = 0
        for piece in pieces:
            fill(keys.at[pair], values.at[pair], at, piece[:, k_at], piece[:, v_at])
            at += piece.shape[0]
        for head in range(2):

            def done(acc, peak, index=2 * pair + head):
                acc_out[index] = acc
                peak_out[index] = jnp.broadcast_to(peak, acc.shape)

            jobs.append(
                (
                    lambda lanes=lanes, head=head: split_queries(q[:, lanes], head),
                    keys[pair, head],
                    values[pair, head],
                    done,
                    count,
                )
            )
    attend(jobs, slots)


def middle_attention(q, pieces):
    count, own = q.shape
    heads = own // HEAD_DIM
    return pl.pallas_call(
        middle_kernel,
        out_shape=[shape(heads, count, LANES, dtype=F32)] * 2,
        in_specs=[VMEM] * 9,
        out_specs=[VMEM] * 2,
        scratch_shapes=[
            pltpu.VMEM((2, 2, LANES, GROUP), BF),
            pltpu.VMEM((2, 2, GROUP, LANES), BF),
            pltpu.VMEM((2, count, GROUP), F32),
        ],
        compiler_params=PARAMS,
        cost_estimate=cost(4 * 10**9, 4 * 10**6),
    )(q, *pieces)


def merge_kernel(me, offsets, qf, *refs):
    pieces, accs_in, peaks_in, mid_acc, mid_peak = (
        refs[:8],
        refs[8:10],
        refs[10:12],
        refs[12],
        refs[13],
    )
    outs, (keys, values, slots, acc, peak, done_rows) = refs[14:18], refs[18:]
    left = left_lanes()
    rows = acc.shape[2]
    few = qf.shape[0]

    def blend(pair, head, which, more, more_peak):
        rate = (MID_RATE, FAR_RATE)[which]
        chosen = pl.ds(offsets[2 * pair + head, which], rows // rate, stride=rate)
        a, p = acc.at[pair, head], peak.at[pair, head]
        old, old_peak = a[chosen, :], p[chosen, :]
        top = jnp.maximum(old_peak, more_peak)
        a[chosen, :] = old * jnp.exp2(old_peak - top) + more * jnp.exp2(more_peak - top)
        p[chosen, :] = top

    jobs = []
    for pair in range(2):
        acc[pair] = accs_in[pair][...]
        peak[pair] = peaks_in[pair][...]
        lanes, k_at, v_at = pair_columns(pair)
        at = 0
        for piece in pieces:
            fill(keys.at[pair], values.at[pair], at, piece[:, k_at], piece[:, v_at])
            at += piece.shape[0]
        for head in range(2):

            def done(more, more_peak, pair=pair, head=head):
                blend(pair, head, 0, mid_acc[2 * pair + head], mid_peak[2 * pair + head])
                blend(pair, head, 1, more, jnp.broadcast_to(more_peak, more.shape))

            jobs.append(
                (
                    lambda lanes=lanes, head=head: split_queries(qf[:, lanes], head),
                    keys[pair, head],
                    values[pair, head],
                    done,
                    few,
                )
            )
    attend(jobs, slots)
    for pair in range(2):
        a, b = acc[pair, 0], acc[pair, 1]
        total = pltpu.roll(jnp.where(left, b, a), HEAD_DIM, 1)
        done_rows[:, pair * LANES : (pair + 1) * LANES] = (jnp.where(left, a, b) / total).astype(BF)
    block = outs[0].shape[0]
    for d, out in enumerate(outs):
        at = pl.multiple_of((me[0] ^ d) * block, block)
        out[...] = done_rows[pl.ds(at, block), :]


def merge(me, offsets, qf, pieces, accs, peaks, mid_acc, mid_peak):
    few, own = qf.shape
    rows = accs[0].shape[1]
    return pl.pallas_call(
        merge_kernel,
        out_shape=[shape(rows // 4, own)] * 4,
        in_specs=[SMEM, SMEM] + [VMEM] * 15,
        out_specs=[VMEM] * 4,
        scratch_shapes=[
            pltpu.VMEM((2, 2, LANES, GROUP), BF),
            pltpu.VMEM((2, 2, GROUP, LANES), BF),
            pltpu.VMEM((2, few, GROUP), F32),
            pltpu.VMEM((2, 2, rows, LANES), F32),
            pltpu.VMEM((2, 2, rows, LANES), F32),
            pltpu.VMEM((rows, own), BF),
        ],
        compiler_params=PARAMS,
        cost_estimate=cost(2 * 10**9, 9 * 10**6),
    )(me, offsets, qf, *pieces, *accs, *peaks, mid_acc, mid_peak)


def out_kernel(me, a0, a1, a2, a3, weight, *outs):
    depth = a0.shape[1]
    for d, out in enumerate(outs):
        columns = pl.ds(pl.multiple_of((me[0] ^ d) * depth, depth), depth)
        total = None
        for e, part in enumerate((a0, a1, a2, a3)):
            rows = pl.ds(pl.multiple_of((me[0] ^ e) * depth, depth), depth)
            term = jnp.dot(part[...], weight[rows, columns], preferred_element_type=F32)
            total = term if total is None else total + term
        out[...] = total.astype(BF)


def project_out(me, parts, weight):
    rows, own = parts[0].shape
    return pl.pallas_call(
        out_kernel,
        out_shape=[shape(rows, own)] * 4,
        in_specs=[SMEM] + [VMEM] * 5,
        out_specs=[VMEM] * 4,
        compiler_params=PARAMS,
        cost_estimate=cost(10**9, 3 * 10**6),
    )(me, *parts, weight)


def place_kernel(me, b0, b1, b2, b3, out):
    block = b0.shape[0]
    for d, part in enumerate((b0, b1, b2, b3)):
        out[pl.ds(pl.multiple_of((me[0] ^ d) * block, block), block), :] = part[...]


def place(me, parts):
    rows, own = parts[0].shape
    return pl.pallas_call(
        place_kernel,
        out_shape=shape(4 * rows, own),
        in_specs=[SMEM] + [VMEM] * 4,
        out_specs=VMEM,
        compiler_params=PARAMS,
    )(me, *parts)


def seg_move(array, target):
    pairs = []
    for i in range(64):
        x, z, core = i // 16, i // 2 % 8, i % 2
        x, z, core = target(x, z, core)
        pairs.append((i, (x % 4 * 8 + z % 8) * 2 + core))
    return lax.ppermute(array, "seg", pairs)


def swap_core(array):
    return seg_move(array, lambda x, z, core: (x, z, 1 - core))


def near_z(array, distance):
    return seg_move(array, lambda x, z, core: (x, z ^ distance, core))


def both_ways(array, distance):
    return seg_move(array, lambda x, z, core: (x, z + (distance if core == 0 else -distance), core))


def along_x(array, distance):
    return seg_move(array, lambda x, z, core: (x ^ distance, z, core))


def swap_head(array, distance):
    return lax.ppermute(array, "head", [(i, i ^ distance) for i in range(4)])


def stack_kernel(*refs, counts):
    out, at = refs[-1], 0
    for ref, count in zip(refs, counts):
        out[at : at + count, :] = ref[:count, :]
        at += count


def stack(parts, after=None):
    counts = tuple(count for _, count in parts)
    extra = [] if after is None else [after]
    return pl.pallas_call(
        functools.partial(stack_kernel, counts=counts),
        out_shape=shape(sum(counts), parts[0][0].shape[1]),
        in_specs=[VMEM] * len(parts) + [ANY] * len(extra),
        out_specs=VMEM,
        compiler_params=PARAMS,
    )(*[array for array, _ in parts], *extra)


def pass_kernel(*refs):
    del refs


def hold(arrays, after):
    count = len(arrays)
    return pl.pallas_call(
        pass_kernel,
        out_shape=[shape(*a.shape, dtype=a.dtype) for a in arrays],
        in_specs=[ANY] * (count + 1),
        out_specs=[ANY] * count,
        input_output_aliases={i: i for i in range(count)},
        compiler_params=PARAMS,
    )(*arrays, after)


def shards(tokens, norm_gain, qkv_weight, out_weight, offsets):
    me = lax.axis_index("head").astype(jnp.int32).reshape(1)
    q, kv0, kv1, qm, kvm, qf, kvf = project(offsets, tokens, norm_gain, qkv_weight)
    far_rows = kvf.shape[0]
    other0, other1 = swap_core(kv0), swap_core(kv1)
    chip = stack([(kvf, far_rows), (swap_core(kvf), far_rows)])
    one, two = both_ways(chip, 1), both_ways(chip, 2)
    onward = stack([(chip, 2 * far_rows), (one, far_rows)])
    three = both_ways(onward, 3)
    mids = [near_z(kvm, distance) for distance in (1, 2, 3)]
    acc0, peak0 = near_attention(q, 0, kv0, other0, onward)
    line = stack(
        [(kvf, far_rows), (one, 2 * far_rows), (two, 2 * far_rows), (three, 3 * far_rows)], acc0
    )
    columns = [along_x(line, distance) for distance in (1, 2, 3)]
    acc1, peak1 = near_attention(q, 1, kv1, other1, line)
    mids = [kvm, *hold(mids, acc1)]
    mids = mids + [swap_core(piece) for piece in mids]
    fars = [line, *hold(columns, acc1)]
    fars = fars + [swap_core(piece) for piece in fars]
    mid_acc, mid_peak = middle_attention(qm, mids)
    parts = merge(me, offsets, qf, fars, (acc0, acc1), (peak0, peak1), mid_acc, mid_peak)
    parts = [parts[0]] + [swap_head(parts[d], d) for d in (1, 2, 3)]
    parts = project_out(me, parts, out_weight)
    parts = [parts[0]] + [swap_head(parts[d], d) for d in (1, 2, 3)]
    return place(me, parts)


def solution(mesh):
    placed = (P("seg", None), P(), P(None, None, "head"), P(), P("head", None))
    return jax.shard_map(
        shards, mesh=mesh, in_specs=placed, out_specs=P("seg", "head"), check_vma=False
    )
```

```python
import functools

import jax
import jax.numpy as jnp
from jax import lax
from jax.experimental import pallas as pl
from jax.experimental.pallas import tpu as pltpu
from jax.sharding import PartitionSpec as P

HEAD_DIM = 64
MID_RATE = 4
FAR_RATE = 32
GROUP = 2048
EPS = 1e-06
LANES = 128
BF = jnp.bfloat16
F32 = jnp.float32
SCALE = 1.4426950408889634 * HEAD_DIM ** (-0.5)
VMEM = pl.BlockSpec(memory_space=pltpu.VMEM)
SMEM = pl.BlockSpec(memory_space=pltpu.SMEM)
ANY = pl.BlockSpec(memory_space=pl.ANY)
PARAMS = pltpu.CompilerParams(vmem_limit_bytes=56 * 2**20)


def shape(*dims, dtype=BF):
    return jax.ShapeDtypeStruct(dims, dtype)


def left_lanes():
    return lax.broadcasted_iota(jnp.int32, (1, LANES), 1) < HEAD_DIM


def cost(flops, bytes_accessed):
    return pl.CostEstimate(flops=flops, bytes_accessed=bytes_accessed, transcendentals=0)


def offset_of(offsets, head, which):
    return jnp.max(offsets[head : head + 1, which : which + 1])


def project_kernel(offsets, tokens, gain, weight, q_out, kv_out, qm_out, kvm_out, qf_out, kvf_out, held):
    rows = tokens.shape[0]
    x = tokens[...].astype(F32)
    mean_square = jnp.mean(x * x, axis=1, keepdims=True)
    normed = (x * lax.rsqrt(mean_square + EPS) * gain[...].astype(F32)[None, :]).astype(BF)
    for part in range(3):
        y = jnp.dot(normed, weight[part], preferred_element_type=F32)
        yb = y.astype(BF)
        if part == 0:
            q_out[...] = yb
        for pair in range(2):
            lanes = slice(pair * LANES, (pair + 1) * LANES)
            held[2 * part + pair] = y[:, lanes]
            if part > 0:
                c = (2 * pair + part - 1) * LANES
                kv_out[:, c : c + LANES] = yb[:, lanes]
    left = left_lanes()
    for rate, which, q_to, kv_to in ((MID_RATE, 0, qm_out, kvm_out), (FAR_RATE, 1, qf_out, kvf_out)):
        count = rows // rate
        for pair in range(2):
            o0 = offset_of(offsets, 2 * pair, which)
            o1 = offset_of(offsets, 2 * pair + 1, which)
            for part in range(3):
                source = held.at[2 * part + pair]
                a = source[pl.ds(o0, count, stride=rate), :]
                b = source[pl.ds(o1, count, stride=rate), :]
                picked = jnp.where(left, a, b).astype(BF)
                if part == 0:
                    q_to[:, pair * LANES : (pair + 1) * LANES] = picked
                else:
                    c = (2 * pair + part - 1) * LANES
                    kv_to[:, c : c + LANES] = picked


def project(offsets, tokens, gain, weight):
    rows, width = tokens.shape
    own = weight.shape[2]
    block = 512

    def rowed(count, columns):
        return pl.BlockSpec((count, columns), lambda i: (i, 0))

    mid, far = block // MID_RATE, block // FAR_RATE
    return pl.pallas_call(
        project_kernel,
        grid=(rows // block,),
        out_shape=[
            shape(rows, own),
            shape(rows, 2 * own),
            shape(rows // MID_RATE, own),
            shape(rows // MID_RATE, 2 * own),
            shape(rows // FAR_RATE, own),
            shape(rows // FAR_RATE, 2 * own),
        ],
        in_specs=[
            pl.BlockSpec(offsets.shape, lambda i: (0, 0)),
            rowed(block, width),
            pl.BlockSpec((width,), lambda i: (0,)),
            pl.BlockSpec((3, width, own), lambda i: (0, 0, 0)),
        ],
        out_specs=[
            rowed(block, own),
            rowed(block, 2 * own),
            rowed(mid, own),
            rowed(mid, 2 * own),
            rowed(far, own),
            rowed(far, 2 * own),
        ],
        scratch_shapes=[pltpu.VMEM((6, block, LANES), F32)],
        compiler_params=PARAMS,
        cost_estimate=cost(2 * 10**9, 6 * 10**6),
    )(offsets, tokens, gain, weight)


def fill(keys, values, at, key_rows, value_rows):
    left = left_lanes()
    count = key_rows.shape[0]
    one = jnp.ones_like(value_rows)
    turned = key_rows.T
    for head in range(2):
        half = turned[head * HEAD_DIM : (head + 1) * HEAD_DIM]
        keys[head, :HEAD_DIM, at : at + count] = half
        keys[head, HEAD_DIM:, at : at + count] = half
    values[0, at : at + count, :] = jnp.where(left, value_rows, one)
    values[1, at : at + count, :] = jnp.where(left, one, value_rows)


def split_queries(q, head):
    left = left_lanes()
    scaled = q.astype(F32) * SCALE
    high = scaled.astype(BF).astype(F32)
    low = scaled - high
    if head == 0:
        both = jnp.where(left, high, pltpu.roll(low, HEAD_DIM, 1))
    else:
        both = jnp.where(left, pltpu.roll(high, HEAD_DIM, 1), low)
    return both.astype(BF)


def attend(jobs, slots):
    def scores(job):
        return jnp.dot(job[0](), job[1], preferred_element_type=F32)

    slots[0, : jobs[0][4]] = scores(jobs[0])
    for i, (_, _, values, done, count) in enumerate(jobs):
        if i + 1 < len(jobs):
            slots[(i + 1) % 2, : jobs[i + 1][4]] = scores(jobs[i + 1])
        s = slots[i % 2, :count]
        peak = jnp.max(s, axis=1, keepdims=True)
        weights = jnp.exp2(s - peak).astype(BF)
        done(jnp.dot(weights, values, preferred_element_type=F32), peak)


def normalised(a, b):
    left = left_lanes()
    total = pltpu.roll(jnp.where(left, b, a), HEAD_DIM, 1)
    return (jnp.where(left, a, b) / total).astype(BF)


def near_kernel(offsets, q, own, theirs, *refs, pair):
    before = refs[0] if pair else None
    refs = refs[1 + pair :]
    out, mid_acc, mid_peak, far_acc, far_peak, acc, peak, keys, values, queries, slots = refs
    rows = q.shape[0]
    block = slots.shape[1]
    for i, kv in enumerate((own, theirs)):
        fill(keys, values, i * rows, kv[:, :LANES], kv[:, LANES:])
    jobs = []
    for head in range(2):
        queries[head] = split_queries(q[...], head)
        for r in range(rows // block):
            at = slice(r * block, (r + 1) * block)

            def done(more, more_peak, head=head, at=at):
                acc[head, at, :] = more
                peak[head, at, :] = jnp.broadcast_to(more_peak, more.shape)

            jobs.append(
                (lambda head=head, at=at: queries[head, at, :], keys[head], values[head], done, block)
            )
    attend(jobs, slots)
    result = normalised(acc[0], acc[1])
    if pair:
        out[:rows, :LANES] = before[...]
        out[:rows, LANES:] = result
        heads = offsets.shape[0]
        row = lax.broadcasted_iota(jnp.int32, (out.shape[0] - rows, out.shape[1]), 0)
        told = jnp.zeros(row.shape, F32)
        for head in range(heads):
            for which in range(2):
                value = offset_of(offsets, head, which).astype(F32)
                told = jnp.where(row == 2 * head + which, value, told)
        out[rows:, :] = told.astype(BF)
    else:
        out[...] = result
    for head in range(2):
        for rate, which, acc_to, peak_to in (
            (MID_RATE, 0, mid_acc, mid_peak),
            (FAR_RATE, 1, far_acc, far_peak),
        ):
            o = offset_of(offsets, 2 * pair + head, which)
            chosen = pl.ds(o, rows // rate, stride=rate)
            acc_to[head] = acc.at[head][chosen, :]
            peak_to[head] = peak.at[head][chosen, :]


def near_attention(offsets, q, pair, own, theirs, after, before=None):
    rows, width = q.shape
    block = 256
    mid, far = rows // MID_RATE, rows // FAR_RATE
    first = shape(rows + 16, width) if pair else shape(rows, LANES)

    def whole(s):
        return pl.BlockSpec(s.shape, lambda i: (0,) * len(s.shape))

    outs = [first] + [shape(2, count, LANES, dtype=F32) for count in (mid, mid, far, far)]
    extra = [before, after] if pair else [after]
    return pl.pallas_call(
        functools.partial(near_kernel, pair=pair),
        grid=(1,),
        out_shape=outs,
        in_specs=[
            whole(offsets),
            pl.BlockSpec((rows, LANES), lambda i: (0, pair)),
            pl.BlockSpec((rows, 2 * LANES), lambda i: (0, pair)),
            pl.BlockSpec((rows, 2 * LANES), lambda i: (0, pair)),
        ]
        + ([whole(before), ANY] if pair else [ANY]),
        out_specs=[whole(s) for s in outs],
        scratch_shapes=[
            pltpu.VMEM((2, rows, LANES), F32),
            pltpu.VMEM((2, rows, LANES), F32),
            pltpu.VMEM((2, LANES, GROUP), BF),
            pltpu.VMEM((2, GROUP, LANES), BF),
            pltpu.VMEM((2, rows, LANES), BF),
            pltpu.VMEM((2, block, GROUP), F32),
        ],
        compiler_params=PARAMS,
        cost_estimate=cost(8 * 10**9, 4 * 10**6),
    )(offsets, q, own, theirs, *extra)


def pair_columns(pair):
    return (
        slice(pair * LANES, (pair + 1) * LANES),
        slice(2 * pair * LANES, (2 * pair + 1) * LANES),
        slice((2 * pair + 1) * LANES, (2 * pair + 2) * LANES),
    )


def blend(old, old_peak, more, more_peak):
    top = jnp.maximum(old_peak, more_peak)
    return old * jnp.exp2(old_peak - top) + more * jnp.exp2(more_peak - top), top


def middle_kernel(q, *refs, count):
    pieces, near_acc, near_peak = refs[:count], refs[count : count + 2], refs[count + 2 : count + 4]
    acc_out, peak_out, keys, values, slots = refs[count + 4 :]
    rows = q.shape[0]
    jobs = []
    for pair in range(2):
        lanes, k_at, v_at = pair_columns(pair)
        at = 0
        for piece in pieces:
            fill(keys.at[pair], values.at[pair], at, piece[:, k_at], piece[:, v_at])
            at += piece.shape[0]
        for head in range(2):

            def done(acc, peak, pair=pair, head=head):
                new, top = blend(near_acc[pair][head], near_peak[pair][head], acc, peak)
                acc_out[2 * pair + head] = new
                peak_out[2 * pair + head] = top

            jobs.append(
                (
                    lambda lanes=lanes, head=head: split_queries(q[:, lanes], head),
                    keys[pair, head],
                    values[pair, head],
                    done,
                    rows,
                )
            )
    attend(jobs, slots)


def middle_attention(q, pieces, near_acc, near_peak):
    rows, own = q.shape
    heads = own // HEAD_DIM
    return pl.pallas_call(
        functools.partial(middle_kernel, count=len(pieces)),
        out_shape=[shape(heads, rows, LANES, dtype=F32)] * 2,
        in_specs=[VMEM] * (5 + len(pieces)),
        out_specs=[VMEM] * 2,
        scratch_shapes=[
            pltpu.VMEM((2, 2, LANES, GROUP), BF),
            pltpu.VMEM((2, 2, GROUP, LANES), BF),
            pltpu.VMEM((2, rows, GROUP), F32),
        ],
        compiler_params=PARAMS,
        cost_estimate=cost(4 * 10**9, 4 * 10**6),
    )(q, *pieces, *near_acc, *near_peak)


def far_kernel(offsets, qf, *refs, count):
    pieces, (near_acc, near_peak) = refs[:count], (refs[count : count + 2], refs[count + 2 : count + 4])
    mid_acc, mid_peak, out, keys, values, slots, acc, peak, far_rows = refs[count + 4 :]
    mid, few = mid_acc.shape[1], qf.shape[0]
    acc[...] = mid_acc[...]
    peak[...] = mid_peak[...]
    jobs = []
    for pair in range(2):
        lanes, k_at, v_at = pair_columns(pair)
        at = 0
        for piece in pieces:
            fill(keys.at[pair], values.at[pair], at, piece[:, k_at], piece[:, v_at])
            at += piece.shape[0]
        for head in range(2):

            def done(more, more_peak, pair=pair, head=head):
                index = 2 * pair + head
                o_mid, o_far = offset_of(offsets, index, 0), offset_of(offsets, index, 1)
                shared = lax.rem(o_far, MID_RATE) == o_mid
                chosen = pl.ds(
                    lax.div(o_far, MID_RATE), few, stride=FAR_RATE // MID_RATE
                )
                held, held_peak = acc.at[index][chosen, :], peak.at[index][chosen, :]
                old = jnp.where(shared, held, near_acc[pair][head])
                old_peak = jnp.where(shared, held_peak, near_peak[pair][head])
                new, top = blend(old, old_peak, more, more_peak)
                acc.at[index][chosen, :] = jnp.where(shared, new, held)
                far_rows[index] = new

            jobs.append(
                (
                    lambda lanes=lanes, head=head: split_queries(qf[:, lanes], head),
                    keys[pair, head],
                    values[pair, head],
                    done,
                    few,
                )
            )
    attend(jobs, slots)
    for pair in range(2):
        lanes = pair_columns(pair)[0]
        out[:mid, lanes] = normalised(acc[2 * pair], acc[2 * pair + 1])
        out[mid:, lanes] = normalised(far_rows[2 * pair], far_rows[2 * pair + 1])


def far_attention(offsets, qf, pieces, near_acc, near_peak, mid_acc, mid_peak):
    few, own = qf.shape
    heads, mid = mid_acc.shape[:2]
    return pl.pallas_call(
        functools.partial(far_kernel, count=len(pieces)),
        out_shape=shape(mid + few, own),
        in_specs=[VMEM] * (8 + len(pieces)),
        out_specs=VMEM,
        scratch_shapes=[
            pltpu.VMEM((2, 2, LANES, GROUP), BF),
            pltpu.VMEM((2, 2, GROUP, LANES), BF),
            pltpu.VMEM((2, few, GROUP), F32),
            pltpu.VMEM((heads, mid, LANES), F32),
            pltpu.VMEM((heads, mid, LANES), F32),
            pltpu.VMEM((heads, few, LANES), F32),
        ],
        compiler_params=PARAMS,
        cost_estimate=cost(2 * 10**9, 4 * 10**6),
    )(offsets, qf, *pieces, *near_acc, *near_peak, mid_acc, mid_peak)


def out_kernel(me, *refs):
    early, late, weight, out, rows32 = refs[:4], refs[4:8], refs[8], refs[9], refs[10]
    rows, own = out.shape
    left = left_lanes()
    mid = rows // MID_RATE
    for d in range(4):
        for pair in range(2):
            rows32[2 * d + pair] = early[d][:rows, pair * LANES : (pair + 1) * LANES].astype(F32)
        told = early[d][rows:, :].astype(F32)
        for pair in range(2):
            lanes = slice(pair * LANES, (pair + 1) * LANES)
            target = rows32.at[2 * d + pair]
            for which, at, rate in ((0, slice(0, mid), MID_RATE), (1, slice(mid, None), FAR_RATE)):
                new = late[d][at, lanes].astype(F32)
                for head in range(2):
                    index = 2 * (2 * pair + head) + which
                    o = jnp.max(told[index : index + 1, :]).astype(jnp.int32)
                    chosen = pl.ds(o, rows // rate, stride=rate)
                    old = target[chosen, :]
                    target[chosen, :] = jnp.where(left, new, old) if head == 0 else jnp.where(left, old, new)
    block = 256
    for r in range(rows // block):
        at = slice(r * block, (r + 1) * block)
        total = None
        for d in range(4):
            depth = pl.ds(pl.multiple_of((me[0] ^ d) * own, own), own)
            part = jnp.concatenate([rows32[2 * d, at, :], rows32[2 * d + 1, at, :]], axis=1).astype(BF)
            term = jnp.dot(part, weight[depth, :], preferred_element_type=F32)
            total = term if total is None else total + term
        out[at, :] = total.astype(BF)


def project_out(me, early, late, weight):
    width = weight.shape[0]
    own = late[0].shape[1]
    rows = late[0].shape[0] * FAR_RATE // (FAR_RATE // MID_RATE + 1)

    def whole(s):
        return pl.BlockSpec(s.shape, lambda i, me: (0,) * len(s.shape))

    return pl.pallas_call(
        out_kernel,
        out_shape=shape(rows, own),
        grid_spec=pltpu.PrefetchScalarGridSpec(
            num_scalar_prefetch=1,
            grid=(1,),
            in_specs=[whole(a) for a in (*early, *late)]
            + [pl.BlockSpec((width, own), lambda i, me: (0, me[0]))],
            out_specs=pl.BlockSpec((rows, own), lambda i, me: (0, 0)),
            scratch_shapes=[pltpu.VMEM((8, rows, LANES), F32)],
        ),
        compiler_params=PARAMS,
        cost_estimate=cost(10**9, 4 * 10**6),
    )(me, *early, *late, weight)


def seg_move(array, target):
    pairs = []
    for i in range(64):
        x, z, core = i // 16, i // 2 % 8, i % 2
        x, z, core = target(x, z, core)
        pairs.append((i, (x % 4 * 8 + z % 8) * 2 + core))
    return lax.ppermute(array, "seg", pairs)


def swap_core(array):
    return seg_move(array, lambda x, z, core: (x, z, 1 - core))


def near_z(array, distance):
    return seg_move(array, lambda x, z, core: (x, z ^ distance, core))


def in_line(array):
    return seg_move(
        array, lambda x, z, core: (x, z // 4 * 4 + (z + (1 if core == 0 else 3)) % 4, core)
    )


def both_ways(array, distance):
    return seg_move(array, lambda x, z, core: (x, z + (distance if core == 0 else -distance), core))


def along_x(array, distance):
    return seg_move(array, lambda x, z, core: (x ^ distance, z, core))


def swap_head(array, distance):
    return lax.ppermute(array, "head", [(i, i ^ distance) for i in range(4)])


def pass_kernel(*refs):
    del refs


def hold(arrays, after):
    count = len(arrays)
    return pl.pallas_call(
        pass_kernel,
        out_shape=[shape(*a.shape, dtype=a.dtype) for a in arrays],
        in_specs=[ANY] * (count + 1),
        out_specs=[ANY] * count,
        input_output_aliases={i: i for i in range(count)},
        compiler_params=PARAMS,
    )(*arrays, after)


def shards(tokens, norm_gain, qkv_weight, out_weight, offsets):
    me = lax.axis_index("head").astype(jnp.int32).reshape(1)
    q, kv, qm, kvm, qf, kvf = project(offsets, tokens, norm_gain, qkv_weight)
    few = kvf.shape[0]
    chip = jnp.concatenate([kvf, swap_core(kvf)], axis=0)
    other = swap_core(kv)
    kvm_other = swap_core(kvm)
    one, two = both_ways(chip, 1), both_ways(chip, 2)
    onward = jnp.concatenate([chip, one[:few]], axis=0)
    three = both_ways(onward, 3)
    kvm, kvm_other = hold([kvm, kvm_other], onward)
    middle_chip = jnp.concatenate([kvm, kvm_other], axis=0)
    beside, across = in_line(middle_chip), near_z(kvm, 2)
    early, *near0 = near_attention(offsets, q, 0, kv, other, middle_chip)
    line = jnp.concatenate([kvf, *hold([one, two, three], early)], axis=0)
    columns = [along_x(line, distance) for distance in (1, 2, 3)]
    early, *near1 = near_attention(offsets, q, 1, kv, other, line, early)
    beside, across, *columns = hold([beside, across, *columns], early)
    middles = [kvm, kvm_other, beside, across, swap_core(beside), swap_core(across)]
    fars = [line, *columns]
    fars = fars + [swap_core(piece) for piece in fars]
    mid_acc, mid_peak = middle_attention(qm, middles, (near0[0], near1[0]), (near0[1], near1[1]))
    late = far_attention(
        offsets, qf, fars, (near0[2], near1[2]), (near0[3], near1[3]), mid_acc, mid_peak
    )
    earlies = [early] + [swap_head(early, d) for d in (1, 2, 3)]
    lates = [late] + [swap_head(late, d) for d in (1, 2, 3)]
    return project_out(me, earlies, lates, out_weight)


def solution(mesh):
    placed = (P("seg", None), P(), P(None, None, "head"), P(), P("head", None))
    return jax.shard_map(
        shards, mesh=mesh, in_specs=placed, out_specs=P("seg", "head"), check_vma=False
    )
```

```python
import functools

import jax
import jax.numpy as jnp
from jax import lax
from jax.experimental import pallas as pl
from jax.experimental.pallas import tpu as pltpu
from jax.sharding import PartitionSpec as P

HEAD_DIM = 64
MID_RATE = 4
FAR_RATE = 32
GROUP = 2048
EPS = 1e-06
LANES = 128
NOTES = 16
BF = jnp.bfloat16
F32 = jnp.float32
SCALE = 1.4426950408889634 * HEAD_DIM ** (-0.5)
VMEM = pl.BlockSpec(memory_space=pltpu.VMEM)
SMEM = pl.BlockSpec(memory_space=pltpu.SMEM)
ANY = pl.BlockSpec(memory_space=pl.ANY)
HBM = pl.BlockSpec(memory_space=pltpu.HBM)


def shape(*dims, dtype=BF):
    return jax.ShapeDtypeStruct(dims, dtype)


def limit(mebibytes):
    return pltpu.CompilerParams(vmem_limit_bytes=mebibytes * 2**20)


def left_lanes():
    return lax.broadcasted_iota(jnp.int32, (1, LANES), 1) < HEAD_DIM


def cost(flops, bytes_accessed):
    return pl.CostEstimate(flops=flops, bytes_accessed=bytes_accessed, transcendentals=0)


def offset_of(offsets, head, which):
    return jnp.max(offsets[which : which + 1, head : head + 1])


def project_kernel(
    offsets, tokens, gain, weight, q_out, kv_out, qm_out, kvm_out, qf_out, kvf_out, x, w, held, sems
):
    rows = tokens.shape[0]
    block = 256
    blocks = rows // block
    copies = [
        pltpu.make_async_copy(tokens.at[pl.ds(r * block, block), :], x.at[pl.ds(r * block, block), :], sems.at[r])
        for r in range(blocks)
    ]
    weights = [pltpu.make_async_copy(weight.at[i], w.at[i], sems.at[blocks + i]) for i in range(3)]
    for copy in [copies[0], *weights, *copies[1:]]:
        copy.start()
    scale = gain[...].astype(F32)[None, :]
    for r in range(blocks):
        at = slice(r * block, (r + 1) * block)
        copies[r].wait()
        rows32 = x[at, :].astype(F32)
        mean_square = jnp.mean(rows32 * rows32, axis=1, keepdims=True)
        normed = (rows32 * lax.rsqrt(mean_square + EPS) * scale).astype(BF)
        for part in range(3):
            if r == 0:
                weights[part].wait()
            y = jnp.dot(normed, w[part], preferred_element_type=F32)
            yb = y.astype(BF)
            if part == 0:
                q_out[at, :] = yb
            for pair in range(2):
                lanes = slice(pair * LANES, (pair + 1) * LANES)
                held[2 * part + pair, at, :] = y[:, lanes]
                if part > 0:
                    c = (2 * pair + part - 1) * LANES
                    kv_out[at, c : c + LANES] = yb[:, lanes]
    left = left_lanes()
    for rate, which, q_to, kv_to in ((MID_RATE, 0, qm_out, kvm_out), (FAR_RATE, 1, qf_out, kvf_out)):
        count = rows // rate
        for pair in range(2):
            o0 = offset_of(offsets, 2 * pair, which)
            o1 = offset_of(offsets, 2 * pair + 1, which)
            for part in range(3):
                source = held.at[2 * part + pair]
                a = source[pl.ds(o0, count, stride=rate), :]
                b = source[pl.ds(o1, count, stride=rate), :]
                picked = jnp.where(left, a, b).astype(BF)
                if part == 0:
                    q_to[:, pair * LANES : (pair + 1) * LANES] = picked
                else:
                    c = (2 * pair + part - 1) * LANES
                    kv_to[:, c : c + LANES] = picked


def project(offsets, tokens, gain, weight):
    rows, width = tokens.shape
    own = weight.shape[2]
    return pl.pallas_call(
        project_kernel,
        out_shape=[
            shape(rows, own),
            shape(rows, 2 * own),
            shape(rows // MID_RATE, own),
            shape(rows // MID_RATE, 2 * own),
            shape(rows // FAR_RATE, own),
            shape(rows // FAR_RATE, 2 * own),
        ],
        in_specs=[VMEM, HBM, VMEM, HBM],
        out_specs=[VMEM] * 6,
        scratch_shapes=[
            pltpu.VMEM((rows, width), BF),
            pltpu.VMEM((3, width, own), BF),
            pltpu.VMEM((6, rows, LANES), F32),
            pltpu.SemaphoreType.DMA((8,)),
        ],
        compiler_params=limit(32),
        cost_estimate=cost(2 * 10**9, 6 * 10**6),
    )(offsets, tokens, gain, weight)


def fill(keys, values, at, key_rows, value_rows):
    left = left_lanes()
    count = key_rows.shape[0]
    one = jnp.ones_like(value_rows)
    turned = key_rows.T
    for head in range(2):
        half = turned[head * HEAD_DIM : (head + 1) * HEAD_DIM]
        keys[head, :HEAD_DIM, at : at + count] = half
        keys[head, HEAD_DIM:, at : at + count] = half
    values[0, at : at + count, :] = jnp.where(left, value_rows, one)
    values[1, at : at + count, :] = jnp.where(left, one, value_rows)


def split_queries(q, head):
    left = left_lanes()
    scaled = q.astype(F32) * SCALE
    high = scaled.astype(BF).astype(F32)
    low = scaled - high
    if head == 0:
        both = jnp.where(left, high, pltpu.roll(low, HEAD_DIM, 1))
    else:
        both = jnp.where(left, pltpu.roll(high, HEAD_DIM, 1), low)
    return both.astype(BF)


def attend(jobs, slots):
    def scores(job):
        return jnp.dot(job[0](), job[1], preferred_element_type=F32)

    slots[0, : jobs[0][4]] = scores(jobs[0])
    for i, (_, _, values, done, count) in enumerate(jobs):
        if i + 1 < len(jobs):
            slots[(i + 1) % 2, : jobs[i + 1][4]] = scores(jobs[i + 1])
        s = slots[i % 2, :count]
        peak = jnp.max(s, axis=1, keepdims=True)
        weights = jnp.exp2(s - peak).astype(BF)
        done(jnp.dot(weights, values, preferred_element_type=F32), peak)


def normalised(a, b):
    left = left_lanes()
    total = pltpu.roll(jnp.where(left, b, a), HEAD_DIM, 1)
    return (jnp.where(left, a, b) / total).astype(BF)


def near_kernel(offsets, q, own, theirs, *refs, pair):
    before = refs[0] if pair else None
    refs = refs[1 + pair :]
    out, mid_acc, mid_peak, far_acc, far_peak, acc, peak, keys, values, queries, slots = refs
    rows = q.shape[0]
    block = slots.shape[1]
    for i, kv in enumerate((own, theirs)):
        fill(keys, values, i * rows, kv[:, :LANES], kv[:, LANES:])
    jobs = []
    for head in range(2):
        queries[head] = split_queries(q[...], head)
        for r in range(rows // block):
            at = slice(r * block, (r + 1) * block)

            def done(more, more_peak, head=head, at=at):
                acc[head, at, :] = more
                peak[head, at, :] = jnp.broadcast_to(more_peak, more.shape)

            jobs.append(
                (lambda head=head, at=at: queries[head, at, :], keys[head], values[head], done, block)
            )
    attend(jobs, slots)
    result = normalised(acc[0], acc[1])
    if pair:
        notes = out.shape[0] - rows
        out[notes:, :LANES] = before[...]
        out[notes:, LANES:] = result
        heads = offsets.shape[1]
        row = lax.broadcasted_iota(jnp.int32, (notes, out.shape[1]), 0)
        told = jnp.zeros(row.shape, F32)
        for head in range(heads):
            for which in range(2):
                value = offset_of(offsets, head, which).astype(F32)
                told = jnp.where(row == 2 * head + which, value, told)
        out[:notes, :] = told.astype(BF)
    else:
        out[...] = result
    for head in range(2):
        for rate, which, acc_to, peak_to in (
            (MID_RATE, 0, mid_acc, mid_peak),
            (FAR_RATE, 1, far_acc, far_peak),
        ):
            o = offset_of(offsets, 2 * pair + head, which)
            chosen = pl.ds(o, rows // rate, stride=rate)
            acc_to[head] = acc.at[head][chosen, :]
            peak_to[head] = peak.at[head][chosen, :]


def near_attention(offsets, q, pair, own, theirs, after, before=None):
    rows, width = q.shape
    block = 256
    mid, far = rows // MID_RATE, rows // FAR_RATE
    first = shape(NOTES + rows, width) if pair else shape(rows, LANES)

    def whole(s):
        return pl.BlockSpec(s.shape, lambda i: (0,) * len(s.shape))

    outs = [first] + [shape(2, count, LANES, dtype=F32) for count in (mid, mid, far, far)]
    extra = [before, after] if pair else [after]
    return pl.pallas_call(
        functools.partial(near_kernel, pair=pair),
        grid=(1,),
        out_shape=outs,
        in_specs=[
            whole(offsets),
            pl.BlockSpec((rows, LANES), lambda i: (0, pair)),
            pl.BlockSpec((rows, 2 * LANES), lambda i: (0, pair)),
            pl.BlockSpec((rows, 2 * LANES), lambda i: (0, pair)),
        ]
        + ([whole(before), ANY] if pair else [ANY]),
        out_specs=[whole(s) for s in outs],
        scratch_shapes=[
            pltpu.VMEM((2, rows, LANES), F32),
            pltpu.VMEM((2, rows, LANES), F32),
            pltpu.VMEM((2, LANES, GROUP), BF),
            pltpu.VMEM((2, GROUP, LANES), BF),
            pltpu.VMEM((2, rows, LANES), BF),
            pltpu.VMEM((2, block, GROUP), F32),
        ],
        compiler_params=limit(28),
        cost_estimate=cost(8 * 10**9, 4 * 10**6),
    )(offsets, q, own, theirs, *extra)


def pair_columns(pair):
    return (
        slice(pair * LANES, (pair + 1) * LANES),
        slice(2 * pair * LANES, (2 * pair + 1) * LANES),
        slice((2 * pair + 1) * LANES, (2 * pair + 2) * LANES),
    )


def blend(old, old_peak, more, more_peak):
    top = jnp.maximum(old_peak, more_peak)
    return old * jnp.exp2(old_peak - top) + more * jnp.exp2(more_peak - top), top


def fetch(pieces, landed, sems):
    started, at = [], 0
    for i, piece in enumerate(pieces):
        rows = piece.shape[0]
        copy = pltpu.make_async_copy(piece, landed.at[pl.ds(at, rows), :], sems.at[i])
        copy.start()
        started.append((at, rows, copy))
        at += rows
    return started


def fill_pieces(started, landed, keys, values):
    for at, rows, copy in started:
        copy.wait()
        for pair in range(2):
            _, k_at, v_at = pair_columns(pair)
            fill(
                keys.at[pair],
                values.at[pair],
                at,
                landed[at : at + rows, k_at],
                landed[at : at + rows, v_at],
            )


def middle_kernel(q, *refs, count):
    pieces, near_acc, near_peak = refs[:count], refs[count : count + 2], refs[count + 2 : count + 4]
    acc_out, peak_out, keys, values, slots, landed, sems = refs[count + 4 :]
    fill_pieces(fetch(pieces, landed, sems), landed, keys, values)
    rows = q.shape[0]
    jobs = []
    for pair in range(2):
        lanes = pair_columns(pair)[0]
        for head in range(2):

            def done(acc, peak, pair=pair, head=head):
                new, top = blend(near_acc[pair][head], near_peak[pair][head], acc, peak)
                acc_out[2 * pair + head] = new
                peak_out[2 * pair + head] = top

            jobs.append(
                (
                    lambda lanes=lanes, head=head: split_queries(q[:, lanes], head),
                    keys[pair, head],
                    values[pair, head],
                    done,
                    rows,
                )
            )
    attend(jobs, slots)


def middle_attention(q, pieces, near_acc, near_peak):
    rows, own = q.shape
    heads = own // HEAD_DIM
    return pl.pallas_call(
        functools.partial(middle_kernel, count=len(pieces)),
        out_shape=[shape(heads, rows, LANES, dtype=F32)] * 2,
        in_specs=[VMEM] + [ANY] * len(pieces) + [VMEM] * 4,
        out_specs=[VMEM] * 2,
        scratch_shapes=[
            pltpu.VMEM((2, 2, LANES, GROUP), BF),
            pltpu.VMEM((2, 2, GROUP, LANES), BF),
            pltpu.VMEM((2, rows, GROUP), F32),
            pltpu.VMEM((GROUP, 2 * own), BF),
            pltpu.SemaphoreType.DMA((len(pieces),)),
        ],
        compiler_params=limit(24),
        cost_estimate=cost(10**6, 10**4),
    )(q, *pieces, *near_acc, *near_peak)


def far_kernel(offsets, qf, *refs, count):
    pieces, (near_acc, near_peak) = refs[:count], (refs[count : count + 2], refs[count + 2 : count + 4])
    mid_acc, mid_peak, out, keys, values, slots, acc, peak, far_rows, landed, sems = refs[count + 4 :]
    started = fetch(pieces, landed, sems)
    mid, few = mid_acc.shape[1], qf.shape[0]
    acc[...] = mid_acc[...]
    peak[...] = mid_peak[...]
    fill_pieces(started, landed, keys, values)
    jobs = []
    for pair in range(2):
        lanes = pair_columns(pair)[0]
        for head in range(2):

            def done(more, more_peak, pair=pair, head=head):
                index = 2 * pair + head
                o_mid, o_far = offset_of(offsets, index, 0), offset_of(offsets, index, 1)
                shared = lax.rem(o_far, MID_RATE) == o_mid
                chosen = pl.ds(
                    lax.div(o_far, MID_RATE), few, stride=FAR_RATE // MID_RATE
                )
                held, held_peak = acc.at[index][chosen, :], peak.at[index][chosen, :]
                old = jnp.where(shared, held, near_acc[pair][head])
                old_peak = jnp.where(shared, held_peak, near_peak[pair][head])
                new, top = blend(old, old_peak, more, more_peak)
                acc.at[index][chosen, :] = jnp.where(shared, new, held)
                far_rows[index] = new

            jobs.append(
                (
                    lambda lanes=lanes, head=head: split_queries(qf[:, lanes], head),
                    keys[pair, head],
                    values[pair, head],
                    done,
                    few,
                )
            )
    attend(jobs, slots)
    for pair in range(2):
        lanes = pair_columns(pair)[0]
        out[:mid, lanes] = normalised(acc[2 * pair], acc[2 * pair + 1])
        out[mid:, lanes] = normalised(far_rows[2 * pair], far_rows[2 * pair + 1])


def far_attention(offsets, qf, pieces, near_acc, near_peak, mid_acc, mid_peak):
    few, own = qf.shape
    heads, mid = mid_acc.shape[:2]
    return pl.pallas_call(
        functools.partial(far_kernel, count=len(pieces)),
        out_shape=shape(mid + few, own),
        in_specs=[VMEM] * 2 + [ANY] * len(pieces) + [VMEM] * 6,
        out_specs=VMEM,
        scratch_shapes=[
            pltpu.VMEM((2, 2, LANES, GROUP), BF),
            pltpu.VMEM((2, 2, GROUP, LANES), BF),
            pltpu.VMEM((2, few, GROUP), F32),
            pltpu.VMEM((heads, mid, LANES), F32),
            pltpu.VMEM((heads, mid, LANES), F32),
            pltpu.VMEM((heads, few, LANES), F32),
            pltpu.VMEM((GROUP, 2 * own), BF),
            pltpu.SemaphoreType.DMA((len(pieces),)),
        ],
        compiler_params=limit(20),
        cost_estimate=cost(10**6, 10**4),
    )(offsets, qf, *pieces, *near_acc, *near_peak, mid_acc, mid_peak)


def out_kernel(me, own, back, ahead, top, bottom, *refs):
    lates, weight, out, early, late, w, rows32, sems = refs[:4], *refs[4:]
    rows, width = out.shape
    left = left_lanes()
    mid = rows // MID_RATE
    half = top.shape[0]
    moves = [
        (own, early.at[0]),
        (back, early.at[1]),
        (ahead, early.at[2]),
        (top, early.at[3, pl.ds(0, half), :]),
        (bottom, early.at[3, pl.ds(half, bottom.shape[0]), :]),
    ]
    moves += [(lates[d], late.at[d]) for d in range(4)]
    moves.append((weight.at[:, pl.ds(pl.multiple_of(me[0] * width, width), width)], w))
    copies = [pltpu.make_async_copy(a, b, sems.at[i]) for i, (a, b) in enumerate(moves)]
    for copy in copies:
        copy.start()
    for d in range(4):
        copies[d].wait()
        if d == 3:
            copies[4].wait()
        for pair in range(2):
            rows32[2 * d + pair] = early[d, NOTES:, pair * LANES : (pair + 1) * LANES].astype(F32)
        told = early[d, :NOTES, :].astype(F32)
        copies[5 + d].wait()
        for pair in range(2):
            lanes = slice(pair * LANES, (pair + 1) * LANES)
            target = rows32.at[2 * d + pair]
            for which, at, rate in (
                (0, slice(0, mid), MID_RATE),
                (1, slice(mid, mid + rows // FAR_RATE), FAR_RATE),
            ):
                new = late[d, at, lanes].astype(F32)
                for head in range(2):
                    index = 2 * (2 * pair + head) + which
                    o = jnp.max(told[index : index + 1, :]).astype(jnp.int32)
                    chosen = pl.ds(o, rows // rate, stride=rate)
                    old = target[chosen, :]
                    target[chosen, :] = jnp.where(left, new, old) if head == 0 else jnp.where(left, old, new)
    copies[9].wait()
    block = 256
    for r in range(rows // block):
        at = slice(r * block, (r + 1) * block)
        total = None
        for d, step in enumerate((0, 3, 1, 2)):
            depth = pl.ds(pl.multiple_of(lax.rem(me[0] + step, 4) * width, width), width)
            part = jnp.concatenate([rows32[2 * d, at, :], rows32[2 * d + 1, at, :]], axis=1).astype(BF)
            term = jnp.dot(part, w[depth, :], preferred_element_type=F32)
            total = term if total is None else total + term
        out[at, :] = total.astype(BF)


def project_out(me, early, late, weight):
    width = weight.shape[0]
    own = late[0].shape[1]
    rows = early[0].shape[0] - NOTES
    return pl.pallas_call(
        out_kernel,
        out_shape=shape(rows, own),
        in_specs=[SMEM] + [ANY] * 9 + [HBM],
        out_specs=VMEM,
        scratch_shapes=[
            pltpu.VMEM((4, NOTES + rows, own), BF),
            pltpu.VMEM((4, *late[0].shape), BF),
            pltpu.VMEM((width, own), BF),
            pltpu.VMEM((8, rows, LANES), F32),
            pltpu.SemaphoreType.DMA((10,)),
        ],
        compiler_params=limit(24),
        cost_estimate=cost(10**9, 4 * 10**6),
    )(me, *early, *late, weight)


def seg_move(array, target):
    pairs = []
    for i in range(64):
        x, z, core = i // 16, i // 2 % 8, i % 2
        x, z, core = target(x, z, core)
        pairs.append((i, (x % 4 * 8 + z % 8) * 2 + core))
    return lax.ppermute(array, "seg", pairs)


def swap_core(array):
    return seg_move(array, lambda x, z, core: (x, z, 1 - core))


def near_z(array, distance):
    return seg_move(array, lambda x, z, core: (x, z ^ distance, core))


def in_line(array):
    return seg_move(
        array, lambda x, z, core: (x, z // 4 * 4 + (z + (1 if core == 0 else 3)) % 4, core)
    )


def both_ways(array, distance):
    return seg_move(array, lambda x, z, core: (x, z + (distance if core == 0 else -distance), core))


def along_x(array, distance):
    return seg_move(array, lambda x, z, core: (x ^ distance, z, core))


def shift_head(array, distance):
    return lax.ppermute(array, "head", [(i, (i + distance) % 4) for i in range(4)])


def assemble_kernel(*refs, plan, count):
    arrays, outs = refs[:count], refs[-len(plan) :]
    for out, parts in zip(outs, plan):
        at = 0
        for index, first, rows in parts:
            out[at : at + rows, :] = arrays[index][first : first + rows, :]
            at += rows


def assemble(wanted, after=None):
    arrays, plan = [], []
    for parts in wanted:
        entry = []
        for array, first, rows in parts:
            entry.append((len(arrays), first, rows))
            arrays.append(array)
        plan.append(tuple(entry))
    extra = [] if after is None else [after]
    return pl.pallas_call(
        functools.partial(assemble_kernel, plan=tuple(plan), count=len(arrays)),
        out_shape=[
            shape(sum(part[2] for part in parts), parts[0][0].shape[1]) for parts in wanted
        ],
        in_specs=[VMEM] * len(arrays) + [ANY] * len(extra),
        out_specs=[VMEM] * len(wanted),
        compiler_params=limit(8),
    )(*arrays, *extra)


def pass_kernel(*refs):
    del refs


def hold(arrays, after):
    count = len(arrays)
    return pl.pallas_call(
        pass_kernel,
        out_shape=[shape(*a.shape, dtype=a.dtype) for a in arrays],
        in_specs=[ANY] * (count + 1),
        out_specs=[ANY] * count,
        input_output_aliases={i: i for i in range(count)},
        compiler_params=limit(2),
    )(*arrays, after)


def shards(tokens, norm_gain, qkv_weight, out_weight, offsets):
    me = lax.axis_index("head").astype(jnp.int32).reshape(1)
    offsets = offsets.T
    q, kv, qm, kvm, qf, kvf = project(offsets, tokens, norm_gain, qkv_weight)
    few, some = kvf.shape[0], kvm.shape[0]
    (chip,) = assemble([[(kvf, 0, few), (swap_core(kvf), 0, few)]])
    one, two = both_ways(chip, 1), both_ways(chip, 2)
    kv, kvm = hold([kv, kvm], chip)
    other = swap_core(kv)
    kvm_other = swap_core(kvm)
    (onward,) = assemble([[(chip, 0, 2 * few), (one, 0, few)]])
    three = both_ways(onward, 3)
    (middle_chip,) = assemble([[(kvm, 0, some), (kvm_other, 0, some)]], onward)
    beside = in_line(middle_chip)
    early, *near0 = near_attention(offsets, q, 0, kv, other, middle_chip)
    (line,) = assemble(
        [[(kvf, 0, few), (one, 0, 2 * few), (two, 0, 2 * few), (three, 0, 3 * few)]], early
    )
    columns = [along_x(line, distance) for distance in (1, 2, 3)]
    early, *near1 = near_attention(offsets, q, 1, kv, other, line, early)
    (beside,) = hold([beside], early)
    (own_half,) = assemble([[(beside, 0, some)]])
    across = in_line(own_half)
    (first,) = hold([columns[0]], early)
    (early,) = hold([early], first)
    back, ahead = shift_head(early, 1), shift_head(early, -1)
    fars = [first, *hold([line, *columns[1:]], early)]
    (beside,) = hold([beside], fars[-1])
    (across,) = hold([across], fars[-1])
    fars = [*fars, *[swap_core(piece) for piece in fars]]
    middles = [kvm, kvm_other, beside, across, swap_core(beside), swap_core(across)]
    mid_acc, mid_peak = middle_attention(qm, middles, (near0[0], near1[0]), (near0[1], near1[1]))
    late = far_attention(
        offsets, qf, fars, (near0[2], near1[2]), (near0[3], near1[3]), mid_acc, mid_peak
    )
    half = NOTES + (early.shape[0] - NOTES) // 2
    top, bottom = assemble([[(back, 0, half)], [(ahead, half, early.shape[0] - half)]], late)
    top, bottom = shift_head(top, 1), shift_head(bottom, -1)
    lates = [late] + [shift_head(late, d) for d in (1, -1, 2)]
    return project_out(me, [early, back, ahead, top, bottom], lates, out_weight)


def solution(mesh):
    placed = (P("seg", None), P(), P(None, None, "head"), P(), P("head", None))
    return jax.shard_map(
        shards, mesh=mesh, in_specs=placed, out_specs=P("seg", "head"), check_vma=False
    )
```

```python
import functools

import jax
import jax.numpy as jnp
from jax import lax
from jax.experimental import pallas as pl
from jax.experimental.pallas import tpu as pltpu
from jax.sharding import PartitionSpec as P

HEAD_DIM = 64
MID_RATE = 4
FAR_RATE = 32
GROUP = 2048
EPS = 1e-06
LANES = 128
NOTES = 16
BF = jnp.bfloat16
F32 = jnp.float32
SCALE = 1.4426950408889634 * HEAD_DIM ** (-0.5)
VMEM = pl.BlockSpec(memory_space=pltpu.VMEM)
SMEM = pl.BlockSpec(memory_space=pltpu.SMEM)
ANY = pl.BlockSpec(memory_space=pl.ANY)
HBM = pl.BlockSpec(memory_space=pltpu.HBM)


def shape(*dims, dtype=BF):
    return jax.ShapeDtypeStruct(dims, dtype)


def limit(mebibytes):
    return pltpu.CompilerParams(vmem_limit_bytes=mebibytes * 2**20)


def left_lanes():
    return lax.broadcasted_iota(jnp.int32, (1, LANES), 1) < HEAD_DIM


AHEAD = pl.CostEstimate(flops=10**12, bytes_accessed=10**6, transcendentals=0)


def offset_of(offsets, head, which):
    return jnp.max(offsets[which : which + 1, head : head + 1])


def project_kernel(
    offsets, tokens, gain, weight, q_out, kv_out, qm_out, kvm_out, qf_out, kvf_out, x, w, held, sems
):
    rows = tokens.shape[0]
    block = 256
    blocks = rows // block
    copies = [
        pltpu.make_async_copy(tokens.at[pl.ds(r * block, block), :], x.at[pl.ds(r * block, block), :], sems.at[r])
        for r in range(blocks)
    ]
    weights = [pltpu.make_async_copy(weight.at[i], w.at[i], sems.at[blocks + i]) for i in range(3)]
    for copy in [copies[0], *weights, *copies[1:]]:
        copy.start()
    scale = gain[...].astype(F32)[None, :]
    for r in range(blocks):
        at = slice(r * block, (r + 1) * block)
        copies[r].wait()
        rows32 = x[at, :].astype(F32)
        mean_square = jnp.mean(rows32 * rows32, axis=1, keepdims=True)
        normed = (rows32 * lax.rsqrt(mean_square + EPS) * scale).astype(BF)
        for part in range(3):
            if r == 0:
                weights[part].wait()
            y = jnp.dot(normed, w[part], preferred_element_type=F32)
            yb = y.astype(BF)
            if part == 0:
                q_out[at, :] = yb
            for pair in range(2):
                lanes = slice(pair * LANES, (pair + 1) * LANES)
                held[2 * part + pair, at, :] = y[:, lanes]
                if part > 0:
                    c = (2 * pair + part - 1) * LANES
                    kv_out[at, c : c + LANES] = yb[:, lanes]
    left = left_lanes()
    for rate, which, q_to, kv_to in ((MID_RATE, 0, qm_out, kvm_out), (FAR_RATE, 1, qf_out, kvf_out)):
        count = rows // rate
        for pair in range(2):
            o0 = offset_of(offsets, 2 * pair, which)
            o1 = offset_of(offsets, 2 * pair + 1, which)
            for part in range(3):
                source = held.at[2 * part + pair]
                a = source[pl.ds(o0, count, stride=rate), :]
                b = source[pl.ds(o1, count, stride=rate), :]
                picked = jnp.where(left, a, b).astype(BF)
                if part == 0:
                    q_to[:, pair * LANES : (pair + 1) * LANES] = picked
                else:
                    c = (2 * pair + part - 1) * LANES
                    kv_to[:, c : c + LANES] = picked


def project(offsets, tokens, gain, weight):
    rows, width = tokens.shape
    own = weight.shape[2]
    return pl.pallas_call(
        project_kernel,
        out_shape=[
            shape(rows, own),
            shape(rows, 2 * own),
            shape(rows // MID_RATE, own),
            shape(rows // MID_RATE, 2 * own),
            shape(rows // FAR_RATE, own),
            shape(rows // FAR_RATE, 2 * own),
        ],
        in_specs=[VMEM, HBM, VMEM, HBM],
        out_specs=[VMEM] * 6,
        scratch_shapes=[
            pltpu.VMEM((rows, width), BF),
            pltpu.VMEM((3, width, own), BF),
            pltpu.VMEM((6, rows, LANES), F32),
            pltpu.SemaphoreType.DMA((8,)),
        ],
        compiler_params=limit(32),
        cost_estimate=AHEAD,
    )(offsets, tokens, gain, weight)


def fill(keys, values, at, key_rows, value_rows):
    left = left_lanes()
    count = key_rows.shape[0]
    one = jnp.ones_like(value_rows)
    turned = key_rows.T
    for head in range(2):
        half = turned[head * HEAD_DIM : (head + 1) * HEAD_DIM]
        keys[head, :HEAD_DIM, at : at + count] = half
        keys[head, HEAD_DIM:, at : at + count] = half
    values[0, at : at + count, :] = jnp.where(left, value_rows, one)
    values[1, at : at + count, :] = jnp.where(left, one, value_rows)


def split_queries(q, head):
    left = left_lanes()
    scaled = q.astype(F32) * SCALE
    high = scaled.astype(BF).astype(F32)
    low = scaled - high
    if head == 0:
        both = jnp.where(left, high, pltpu.roll(low, HEAD_DIM, 1))
    else:
        both = jnp.where(left, pltpu.roll(high, HEAD_DIM, 1), low)
    return both.astype(BF)


def attend(jobs, slots):
    def scores(job):
        return jnp.dot(job[0](), job[1], preferred_element_type=F32)

    slots[0, : jobs[0][4]] = scores(jobs[0])
    for i, (_, _, values, done, count) in enumerate(jobs):
        if i + 1 < len(jobs):
            slots[(i + 1) % 2, : jobs[i + 1][4]] = scores(jobs[i + 1])
        s = slots[i % 2, :count]
        peak = jnp.max(s, axis=1, keepdims=True)
        weights = jnp.exp2(s - peak).astype(BF)
        done(jnp.dot(weights, values, preferred_element_type=F32), peak)


def normalised(a, b, total_a=None, total_b=None):
    left = left_lanes()
    total_a = a if total_a is None else total_a
    total_b = b if total_b is None else total_b
    total = pltpu.roll(jnp.where(left, total_b, total_a), HEAD_DIM, 1)
    return (jnp.where(left, a, b) / total).astype(BF)


def near_kernel(offsets, q, own, theirs, *refs, pair):
    refs = refs[1:]
    out, mid_acc, mid_peak, far_acc, far_peak, acc, peak, keys, values, queries, slots = refs
    rows = q.shape[0]
    block = slots.shape[1]
    for i, kv in enumerate((own, theirs)):
        fill(keys, values, i * rows, kv[:, :LANES], kv[:, LANES:])
    jobs = []
    for head in range(2):
        queries[head] = split_queries(q[...], head)
        for r in range(rows // block):
            at = slice(r * block, (r + 1) * block)

            def done(more, more_peak, head=head, at=at):
                acc[head, at, :] = more
                peak[head, at, :] = jnp.broadcast_to(more_peak, more.shape)

            jobs.append(
                (lambda head=head, at=at: queries[head, at, :], keys[head], values[head], done, block)
            )
    attend(jobs, slots)
    result = normalised(acc[0], acc[1])
    notes = out.shape[0] - rows
    out[notes:, :] = result
    if notes:
        row = lax.broadcasted_iota(jnp.int32, (notes, LANES), 0)
        told = jnp.zeros(row.shape, F32)
        for head in range(offsets.shape[1]):
            for which in range(2):
                value = offset_of(offsets, head, which).astype(F32)
                told = jnp.where(row == 2 * head + which, value, told)
        out[:notes, :] = told.astype(BF)
    for head in range(2):
        for rate, which, acc_to, peak_to in (
            (MID_RATE, 0, mid_acc, mid_peak),
            (FAR_RATE, 1, far_acc, far_peak),
        ):
            o = offset_of(offsets, 2 * pair + head, which)
            chosen = pl.ds(o, rows // rate, stride=rate)
            acc_to[head] = acc.at[head][chosen, :]
            peak_to[head] = peak.at[head][chosen, :]


def near_attention(offsets, q, pair, own, theirs, after):
    rows = q.shape[0]
    block = 256
    mid, far = rows // MID_RATE, rows // FAR_RATE
    first = shape(rows + (0 if pair else NOTES), LANES)

    def whole(s):
        return pl.BlockSpec(s.shape, lambda i: (0,) * len(s.shape))

    outs = [first] + [shape(2, count, LANES, dtype=F32) for count in (mid, mid, far, far)]
    return pl.pallas_call(
        functools.partial(near_kernel, pair=pair),
        grid=(1,),
        out_shape=outs,
        in_specs=[
            whole(offsets),
            pl.BlockSpec((rows, LANES), lambda i: (0, pair)),
            pl.BlockSpec((rows, 2 * LANES), lambda i: (0, pair)),
            pl.BlockSpec((rows, 2 * LANES), lambda i: (0, pair)),
            ANY,
        ],
        out_specs=[whole(s) for s in outs],
        scratch_shapes=[
            pltpu.VMEM((2, rows, LANES), F32),
            pltpu.VMEM((2, rows, LANES), F32),
            pltpu.VMEM((2, LANES, GROUP), BF),
            pltpu.VMEM((2, GROUP, LANES), BF),
            pltpu.VMEM((2, rows, LANES), BF),
            pltpu.VMEM((2, block, GROUP), F32),
        ],
        compiler_params=limit(28),
        cost_estimate=AHEAD,
    )(offsets, q, own, theirs, after)


def pair_columns(pair):
    return (
        slice(pair * LANES, (pair + 1) * LANES),
        slice(2 * pair * LANES, (2 * pair + 1) * LANES),
        slice((2 * pair + 1) * LANES, (2 * pair + 2) * LANES),
    )


def blend(old, old_peak, more, more_peak):
    top = jnp.maximum(old_peak, more_peak)
    return old * jnp.exp2(old_peak - top) + more * jnp.exp2(more_peak - top), top


def fetch(pieces, landed, sems):
    started, at = [], 0
    for i, piece in enumerate(pieces):
        rows = piece.shape[0]
        copy = pltpu.make_async_copy(piece, landed.at[pl.ds(at, rows), :], sems.at[i])
        copy.start()
        started.append((at, rows, copy))
        at += rows
    return started


def fill_pieces(started, landed, keys, values):
    for at, rows, copy in started:
        copy.wait()
        for pair in range(2):
            _, k_at, v_at = pair_columns(pair)
            fill(
                keys.at[pair],
                values.at[pair],
                at,
                landed[at : at + rows, k_at],
                landed[at : at + rows, v_at],
            )


def middle_kernel(q, *refs, count):
    pieces, near_acc, near_peak = refs[:count], refs[count : count + 2], refs[count + 2 : count + 4]
    acc_out, peak_out, keys, values, slots, landed, sems = refs[count + 4 :]
    fill_pieces(fetch(pieces, landed, sems), landed, keys, values)
    rows = q.shape[0]
    jobs = []
    for pair in range(2):
        lanes = pair_columns(pair)[0]
        for head in range(2):

            def done(acc, peak, pair=pair, head=head):
                new, top = blend(near_acc[pair][head], near_peak[pair][head], acc, peak)
                acc_out[2 * pair + head] = new
                peak_out[2 * pair + head] = top

            jobs.append(
                (
                    lambda lanes=lanes, head=head: split_queries(q[:, lanes], head),
                    keys[pair, head],
                    values[pair, head],
                    done,
                    rows,
                )
            )
    attend(jobs, slots)


def middle_attention(q, pieces, near_acc, near_peak):
    rows, own = q.shape
    heads = own // HEAD_DIM
    return pl.pallas_call(
        functools.partial(middle_kernel, count=len(pieces)),
        out_shape=[shape(heads, rows, LANES, dtype=F32)] * 2,
        in_specs=[VMEM] + [ANY] * len(pieces) + [VMEM] * 4,
        out_specs=[VMEM] * 2,
        scratch_shapes=[
            pltpu.VMEM((2, 2, LANES, GROUP), BF),
            pltpu.VMEM((2, 2, GROUP, LANES), BF),
            pltpu.VMEM((2, rows, GROUP), F32),
            pltpu.VMEM((GROUP, 2 * own), BF),
            pltpu.SemaphoreType.DMA((len(pieces),)),
        ],
        compiler_params=limit(24),
        cost_estimate=AHEAD,
    )(q, *pieces, *near_acc, *near_peak)


def far_kernel(offsets, qf, *refs, count):
    pieces, (near_acc, near_peak) = refs[:count], (refs[count : count + 2], refs[count + 2 : count + 4])
    mid_acc, mid_peak, out, keys, values, slots, acc, peak, far_rows, far_total, landed, sems = refs[
        count + 4 :
    ]
    started = fetch(pieces, landed, sems)
    mid, few = mid_acc.shape[1], qf.shape[0]
    acc[...] = mid_acc[...]
    peak[...] = mid_peak[...]
    fill_pieces(started, landed, keys, values)
    jobs = []
    for pair in range(2):
        lanes = pair_columns(pair)[0]
        for head in range(2):

            def done(more, more_peak, pair=pair, head=head):
                index = 2 * pair + head
                o_mid, o_far = offset_of(offsets, index, 0), offset_of(offsets, index, 1)
                shared = lax.rem(o_far, MID_RATE) == o_mid
                chosen = pl.ds(
                    lax.div(o_far, MID_RATE), few, stride=FAR_RATE // MID_RATE
                )
                held, held_peak = acc.at[index][chosen, :], peak.at[index][chosen, :]
                old = jnp.where(shared, held, near_acc[pair][head])
                old_peak = jnp.where(shared, held_peak, near_peak[pair][head])
                new, top = blend(old, old_peak, more, more_peak)
                acc.at[index][chosen, :] = jnp.where(shared, new, held)
                far_rows[index] = jnp.where(shared, 0.0, new)
                far_total[index] = jnp.where(shared, 1.0, new)

            jobs.append(
                (
                    lambda lanes=lanes, head=head: split_queries(qf[:, lanes], head),
                    keys[pair, head],
                    values[pair, head],
                    done,
                    few,
                )
            )
    attend(jobs, slots)
    for pair in range(2):
        lanes = pair_columns(pair)[0]
        out[:mid, lanes] = normalised(acc[2 * pair], acc[2 * pair + 1])
        out[mid:, lanes] = normalised(
            far_rows[2 * pair], far_rows[2 * pair + 1], far_total[2 * pair], far_total[2 * pair + 1]
        )


def far_attention(offsets, qf, pieces, near_acc, near_peak, mid_acc, mid_peak):
    few, own = qf.shape
    heads, mid = mid_acc.shape[:2]
    return pl.pallas_call(
        functools.partial(far_kernel, count=len(pieces)),
        out_shape=shape(mid + few, own),
        in_specs=[VMEM] * 2 + [ANY] * len(pieces) + [VMEM] * 6,
        out_specs=VMEM,
        scratch_shapes=[
            pltpu.VMEM((2, 2, LANES, GROUP), BF),
            pltpu.VMEM((2, 2, GROUP, LANES), BF),
            pltpu.VMEM((2, few, GROUP), F32),
            pltpu.VMEM((heads, mid, LANES), F32),
            pltpu.VMEM((heads, mid, LANES), F32),
            pltpu.VMEM((heads, few, LANES), F32),
            pltpu.VMEM((heads, few, LANES), F32),
            pltpu.VMEM((GROUP, 2 * own), BF),
            pltpu.SemaphoreType.DMA((len(pieces),)),
        ],
        compiler_params=limit(20),
    )(offsets, qf, *pieces, *near_acc, *near_peak, mid_acc, mid_peak)


def told_offset(notes, pair, head, which):
    index = 2 * (2 * pair + head) + which
    return jnp.max(notes[index : index + 1, :]).astype(jnp.int32)


def weight_rows(me, d, pair, width):
    step = (0, 3, 1, 2)[d]
    first = lax.rem(me[0] + step, 4) * width + pair * LANES
    return pl.ds(pl.multiple_of(first, LANES), LANES)


def late_kernel(me, own, back, ahead, across, n0, n1, n2, n3, weight, out, w_out, sem):
    rows, width = out.shape[1], 2 * LANES
    left = left_lanes()
    mid = rows // MID_RATE
    columns = pl.ds(pl.multiple_of(me[0] * width, width), width)
    copy = pltpu.make_async_copy(weight.at[:, columns], w_out, sem)
    copy.start()
    for side in range(2):
        out[side] = jnp.zeros((rows, LANES), F32)
    copy.wait()
    for d, (source, note) in enumerate(zip((own, back, ahead, across), (n0, n1, n2, n3))):
        notes = note[:NOTES, :].astype(F32)
        for pair in range(2):
            late = source[:, pair * LANES : (pair + 1) * LANES]
            zero = jnp.zeros_like(late)
            rows_of = w_out[weight_rows(me, d, pair, width), :]
            for head in range(2):
                part = jnp.where(left, late, zero) if head == 0 else jnp.where(left, zero, late)
                term = jnp.dot(part, rows_of, preferred_element_type=F32)
                for which, at, rate in ((0, 0, MID_RATE), (1, mid, FAR_RATE)):
                    count = rows // rate
                    chosen = pl.ds(told_offset(notes, pair, head, which), count, stride=rate)
                    for side in range(2):
                        target = out.at[side]
                        lanes = slice(side * LANES, (side + 1) * LANES)
                        target[chosen, :] = target[chosen, :] + term[at : at + count, lanes]


def late_product(me, lates, notes, weight, rows):
    depth, own = weight.shape[0], lates[0].shape[1]
    return pl.pallas_call(
        late_kernel,
        out_shape=[shape(2, rows, LANES, dtype=F32), shape(depth, own)],
        in_specs=[SMEM] + [VMEM] * 8 + [ANY],
        out_specs=[VMEM] * 2,
        scratch_shapes=[pltpu.SemaphoreType.DMA],
        compiler_params=limit(16),
    )(me, *lates, *notes, weight)


def final_kernel(me, late, w, *refs, plan, count):
    arrays, (out, rows32) = refs[:count], refs[count:]
    rows, width = out.shape
    left = left_lanes()
    for slot, parts in enumerate(plan):
        d, pair = slot // 2, slot % 2
        target = rows32.at[slot]
        index, first, _ = plan[2 * d][0]
        notes = arrays[index][first : first + NOTES, :].astype(F32)
        at = 0
        for i, (index, first, length) in enumerate(parts):
            skip = NOTES if i == 0 and pair == 0 else 0
            size = length - skip
            target[at : at + size, :] = arrays[index][first + skip : first + length, :].astype(F32)
            at += size
        for which, rate in ((0, MID_RATE), (1, FAR_RATE)):
            for head in range(2):
                chosen = pl.ds(told_offset(notes, pair, head, which), rows // rate, stride=rate)
                old = target[chosen, :]
                target[chosen, :] = jnp.where(left, 0.0, old) if head == 0 else jnp.where(left, old, 0.0)
    block = 256
    for r in range(rows // block):
        at = slice(r * block, (r + 1) * block)
        total = jnp.concatenate([late[0, at, :], late[1, at, :]], axis=1)
        for d in range(4):
            first = weight_rows(me, d, 0, width).start
            rows_of = w[pl.ds(pl.multiple_of(first, width), width), :]
            part = jnp.concatenate([rows32[2 * d, at, :], rows32[2 * d + 1, at, :]], axis=1).astype(BF)
            total = total + jnp.dot(part, rows_of, preferred_element_type=F32)
        out[at, :] = total.astype(BF)


def final_product(me, late, w, pieces):
    arrays, plan = [], []
    for parts in pieces:
        entry = []
        for array, first, length in parts:
            known = [i for i, a in enumerate(arrays) if a is array]
            if not known:
                arrays.append(array)
            entry.append((known[0] if known else len(arrays) - 1, first, length))
        plan.append(tuple(entry))
    rows, own = late.shape[1], w.shape[1]
    return pl.pallas_call(
        functools.partial(final_kernel, plan=tuple(plan), count=len(arrays)),
        out_shape=shape(rows, own),
        in_specs=[SMEM] + [VMEM] * (2 + len(arrays)),
        out_specs=VMEM,
        scratch_shapes=[pltpu.VMEM((8, rows, LANES), F32)],
        compiler_params=limit(24),
    )(me, late, w, *arrays)


def seg_move(array, target):
    pairs = []
    for i in range(64):
        x, z, core = i // 16, i // 2 % 8, i % 2
        x, z, core = target(x, z, core)
        pairs.append((i, (x % 4 * 8 + z % 8) * 2 + core))
    return lax.ppermute(array, "seg", pairs)


def swap_core(array):
    return seg_move(array, lambda x, z, core: (x, z, 1 - core))


def near_z(array, distance):
    return seg_move(array, lambda x, z, core: (x, z ^ distance, core))


def in_line(array):
    return seg_move(
        array, lambda x, z, core: (x, z // 4 * 4 + (z + (1 if core == 0 else 3)) % 4, core)
    )


def both_ways(array, distance):
    return seg_move(array, lambda x, z, core: (x, z + (distance if core == 0 else -distance), core))


def along_x(array, distance):
    return seg_move(array, lambda x, z, core: (x + (distance if core == 0 else -distance), z, core))


def shift_head(array, distance):
    return lax.ppermute(array, "head", [(i, (i + distance) % 4) for i in range(4)])


def assemble_kernel(*refs, plan, count):
    arrays, outs = refs[:count], refs[-len(plan) :]
    for out, parts in zip(outs, plan):
        at = 0
        for index, first, rows in parts:
            out[at : at + rows, :] = arrays[index][first : first + rows, :]
            at += rows


def assemble(wanted, after=None):
    arrays, plan = [], []
    for parts in wanted:
        entry = []
        for array, first, rows in parts:
            entry.append((len(arrays), first, rows))
            arrays.append(array)
        plan.append(tuple(entry))
    extra = [] if after is None else [after]
    return pl.pallas_call(
        functools.partial(assemble_kernel, plan=tuple(plan), count=len(arrays)),
        out_shape=[
            shape(sum(part[2] for part in parts), parts[0][0].shape[1]) for parts in wanted
        ],
        in_specs=[VMEM] * len(arrays) + [ANY] * len(extra),
        out_specs=[VMEM] * len(wanted),
        compiler_params=limit(8),
    )(*arrays, *extra)


def pass_kernel(*refs):
    del refs


def hold(arrays, after, **options):
    count = len(arrays)
    return pl.pallas_call(
        pass_kernel,
        out_shape=[shape(*a.shape, dtype=a.dtype) for a in arrays],
        in_specs=[ANY] * (count + 1),
        out_specs=[ANY] * count,
        input_output_aliases={i: i for i in range(count)},
        compiler_params=limit(2),
        **options,
    )(*arrays, after)


def fence(arrays, after):
    return hold(arrays, after, cost_estimate=AHEAD)


def shards(tokens, norm_gain, qkv_weight, out_weight, offsets):
    me = lax.axis_index("head").astype(jnp.int32).reshape(1)
    offsets = offsets.T
    q, kv, qm, kvm, qf, kvf = project(offsets, tokens, norm_gain, qkv_weight)
    few, some = kvf.shape[0], kvm.shape[0]
    (chip,) = assemble([[(kvf, 0, few), (swap_core(kvf), 0, few)]])
    one, two = both_ways(chip, 1), both_ways(chip, 2)
    kv, kvm = hold([kv, kvm], chip)
    other = swap_core(kv)
    kvm_other = swap_core(kvm)
    (kvm_other,) = fence([kvm_other], chip)
    (middle_chip,) = assemble([[(kvm, 0, some), (kvm_other, 0, some)]])
    beside = in_line(middle_chip)
    (onward,) = assemble([[(chip, 0, 2 * few), (one, 0, few)]], middle_chip)
    three = both_ways(onward, 3)
    early0, *near0 = near_attention(offsets, q, 0, kv, other, onward)
    back0, ahead0 = shift_head(early0, 1), shift_head(early0, -1)
    two, three = hold([two, three], early0)
    (line,) = assemble(
        [[(kvf, 0, few), (one, 0, 2 * few), (two, 0, 2 * few), (three, 0, 3 * few)]]
    )
    line_other = swap_core(line)
    (beside,) = hold([beside], line)
    (own_half,) = assemble([[(beside, 0, some)]])
    across = in_line(own_half)
    (column,) = assemble([[(line, 0, 8 * few), (line_other, 0, 8 * few)]], own_half)
    sides, opposite = along_x(column, 1), along_x(line, 2)
    early1, *near1 = near_attention(offsets, q, 1, kv, other, column)
    rows = early1.shape[0]
    half = rows // 2
    up, down = assemble(
        [
            [(back0, 0, NOTES + half), (early1, 0, rows)],
            [(ahead0, NOTES + half, half), (early1, 0, rows)],
        ]
    )
    back1, ahead1 = shift_head(up, 1), shift_head(down, -1)
    (far_gathered,) = assemble([[(sides, 0, 16 * few), (opposite, 0, 8 * few)]], up)
    (gathered,) = assemble([[(beside, 0, 2 * some), (across, 0, some)]], far_gathered)
    middles = [kvm, kvm_other, gathered, swap_core(gathered)]
    fars = [line, line_other, far_gathered, swap_core(far_gathered)]
    mid_acc, mid_peak = middle_attention(qm, middles, (near0[0], near1[0]), (near0[1], near1[1]))
    late = far_attention(
        offsets, qf, fars, (near0[2], near1[2]), (near0[3], near1[3]), mid_acc, mid_peak
    )
    lates = [late] + [shift_head(late, d) for d in (1, -1, 2)]
    top, bottom = assemble([[(back1, NOTES + half, half)], [(ahead1, 2 * half, half)]], late)
    top, bottom = shift_head(top, 1), shift_head(bottom, -1)
    late_sum, w = late_product(me, lates, [early0, back0, ahead0, back1], out_weight, rows)
    return final_product(
        me,
        late_sum,
        w,
        [
            [(early0, 0, NOTES + rows)],
            [(early1, 0, rows)],
            [(back0, 0, NOTES + rows)],
            [(back1, NOTES + half, rows)],
            [(ahead0, 0, NOTES + rows)],
            [(ahead1, half, rows)],
            [(back1, 0, NOTES + half), (ahead1, 0, half)],
            [(top, 0, half), (bottom, 0, half)],
        ],
    )


def solution(mesh):
    placed = (P("seg", None), P(), P(None, None, "head"), P(), P("head", None))
    return jax.shard_map(
        shards, mesh=mesh, in_specs=placed, out_specs=P("seg", "head"), check_vma=False
    )
```

```python
import functools

import jax
import jax.numpy as jnp
from jax import lax
from jax.experimental import pallas as pl
from jax.experimental.pallas import tpu as pltpu
from jax.sharding import PartitionSpec as P

HEAD_DIM = 64
MID_RATE = 4
FAR_RATE = 32
GROUP = 2048
EPS = 1e-06
LANES = 128
NOTES = 16
BF = jnp.bfloat16
F32 = jnp.float32
SCALE = 1.4426950408889634 * HEAD_DIM ** (-0.5)
VMEM = pl.BlockSpec(memory_space=pltpu.VMEM)
SMEM = pl.BlockSpec(memory_space=pltpu.SMEM)
ANY = pl.BlockSpec(memory_space=pl.ANY)
HBM = pl.BlockSpec(memory_space=pltpu.HBM)


def shape(*dims, dtype=BF):
    return jax.ShapeDtypeStruct(dims, dtype)


def limit(mebibytes):
    return pltpu.CompilerParams(vmem_limit_bytes=mebibytes * 2**20)


def left_lanes():
    return lax.broadcasted_iota(jnp.int32, (1, LANES), 1) < HEAD_DIM


AHEAD = pl.CostEstimate(flops=2 * 10**10, bytes_accessed=10**7, transcendentals=0)


def offset_of(offsets, head, which):
    return jnp.max(offsets[which : which + 1, head : head + 1])


def project_kernel(
    offsets, tokens, gain, weight, q_out, kv_out, qm_out, kvm_out, qf_out, kvf_out, x, w, held, sems
):
    rows = tokens.shape[0]
    block = 256
    blocks = rows // block
    copies = [
        pltpu.make_async_copy(tokens.at[pl.ds(r * block, block), :], x.at[pl.ds(r * block, block), :], sems.at[r])
        for r in range(blocks)
    ]
    weights = [pltpu.make_async_copy(weight.at[i], w.at[i], sems.at[blocks + i]) for i in range(3)]
    for copy in [copies[0], *weights, *copies[1:]]:
        copy.start()
    scale = gain[...].astype(F32)[None, :]
    for r in range(blocks):
        at = slice(r * block, (r + 1) * block)
        copies[r].wait()
        rows32 = x[at, :].astype(F32)
        mean_square = jnp.mean(rows32 * rows32, axis=1, keepdims=True)
        normed = (rows32 * lax.rsqrt(mean_square + EPS) * scale).astype(BF)
        for part in range(3):
            if r == 0:
                weights[part].wait()
            y = jnp.dot(normed, w[part], preferred_element_type=F32)
            yb = y.astype(BF)
            if part == 0:
                q_out[at, :] = yb
            for pair in range(2):
                lanes = slice(pair * LANES, (pair + 1) * LANES)
                held[2 * part + pair, at, :] = y[:, lanes]
                if part > 0:
                    c = (2 * pair + part - 1) * LANES
                    kv_out[at, c : c + LANES] = yb[:, lanes]
    left = left_lanes()
    for rate, which, q_to, kv_to in ((MID_RATE, 0, qm_out, kvm_out), (FAR_RATE, 1, qf_out, kvf_out)):
        count = rows // rate
        for pair in range(2):
            o0 = offset_of(offsets, 2 * pair, which)
            o1 = offset_of(offsets, 2 * pair + 1, which)
            for part in range(3):
                source = held.at[2 * part + pair]
                a = source[pl.ds(o0, count, stride=rate), :]
                b = source[pl.ds(o1, count, stride=rate), :]
                picked = jnp.where(left, a, b).astype(BF)
                if part == 0:
                    q_to[:, pair * LANES : (pair + 1) * LANES] = picked
                else:
                    c = (2 * pair + part - 1) * LANES
                    kv_to[:, c : c + LANES] = picked


def project(offsets, tokens, gain, weight):
    rows, width = tokens.shape
    own = weight.shape[2]
    return pl.pallas_call(
        project_kernel,
        out_shape=[
            shape(rows, own),
            shape(rows, 2 * own),
            shape(rows // MID_RATE, own),
            shape(rows // MID_RATE, 2 * own),
            shape(rows // FAR_RATE, own),
            shape(rows // FAR_RATE, 2 * own),
        ],
        in_specs=[VMEM, HBM, VMEM, HBM],
        out_specs=[VMEM] * 6,
        scratch_shapes=[
            pltpu.VMEM((rows, width), BF),
            pltpu.VMEM((3, width, own), BF),
            pltpu.VMEM((6, rows, LANES), F32),
            pltpu.SemaphoreType.DMA((8,)),
        ],
        compiler_params=limit(51),
        cost_estimate=AHEAD,
    )(offsets, tokens, gain, weight)


def fill(keys, values, at, key_rows, value_rows):
    left = left_lanes()
    count = key_rows.shape[0]
    one = jnp.ones_like(value_rows)
    turned = key_rows.T
    for head in range(2):
        half = turned[head * HEAD_DIM : (head + 1) * HEAD_DIM]
        keys[head, :HEAD_DIM, at : at + count] = half
        keys[head, HEAD_DIM:, at : at + count] = half
    values[0, at : at + count, :] = jnp.where(left, value_rows, one)
    values[1, at : at + count, :] = jnp.where(left, one, value_rows)


def split_queries(q, head):
    left = left_lanes()
    scaled = q.astype(F32) * SCALE
    high = scaled.astype(BF).astype(F32)
    low = scaled - high
    if head == 0:
        both = jnp.where(left, high, pltpu.roll(low, HEAD_DIM, 1))
    else:
        both = jnp.where(left, pltpu.roll(high, HEAD_DIM, 1), low)
    return both.astype(BF)


def attend(jobs, slots):
    def scores(job):
        return jnp.dot(job[0](), job[1], preferred_element_type=F32)

    slots[0, : jobs[0][4]] = scores(jobs[0])
    for i, (_, _, values, done, count) in enumerate(jobs):
        if i + 1 < len(jobs):
            slots[(i + 1) % 2, : jobs[i + 1][4]] = scores(jobs[i + 1])
        s = slots[i % 2, :count]
        peak = jnp.max(s, axis=1, keepdims=True)
        weights = jnp.exp2(s - peak).astype(BF)
        done(jnp.dot(weights, values, preferred_element_type=F32), peak)


def normalised(a, b, total_a=None, total_b=None):
    left = left_lanes()
    total_a = a if total_a is None else total_a
    total_b = b if total_b is None else total_b
    total = pltpu.roll(jnp.where(left, total_b, total_a), HEAD_DIM, 1)
    return (jnp.where(left, a, b) / total).astype(BF)


def near_kernel(offsets, q, own, theirs, *refs, pair):
    refs = refs[1:]
    out, mid_acc, mid_peak, far_acc, far_peak, acc, peak, keys, values, queries, slots = refs
    rows = q.shape[0]
    block = slots.shape[1]
    for i, kv in enumerate((own, theirs)):
        fill(keys, values, i * rows, kv[:, :LANES], kv[:, LANES:])
    jobs = []
    for head in range(2):
        queries[head] = split_queries(q[...], head)
        for r in range(rows // block):
            at = slice(r * block, (r + 1) * block)

            def done(more, more_peak, head=head, at=at):
                acc[head, at, :] = more
                peak[head, at, :] = jnp.broadcast_to(more_peak, more.shape)

            jobs.append(
                (lambda head=head, at=at: queries[head, at, :], keys[head], values[head], done, block)
            )
    attend(jobs, slots)
    result = normalised(acc[0], acc[1])
    out[...] = result
    for head in range(2):
        for rate, which, acc_to, peak_to in (
            (MID_RATE, 0, mid_acc, mid_peak),
            (FAR_RATE, 1, far_acc, far_peak),
        ):
            o = offset_of(offsets, 2 * pair + head, which)
            chosen = pl.ds(o, rows // rate, stride=rate)
            acc_to[head] = acc.at[head][chosen, :]
            peak_to[head] = peak.at[head][chosen, :]


def near_attention(offsets, q, pair, own, theirs, after):
    rows = q.shape[0]
    block = 256
    mid, far = rows // MID_RATE, rows // FAR_RATE
    first = shape(rows, LANES)

    def whole(s):
        return pl.BlockSpec(s.shape, lambda i: (0,) * len(s.shape))

    outs = [first] + [shape(2, count, LANES, dtype=F32) for count in (mid, mid, far, far)]
    return pl.pallas_call(
        functools.partial(near_kernel, pair=pair),
        grid=(1,),
        out_shape=outs,
        in_specs=[
            whole(offsets),
            pl.BlockSpec((rows, LANES), lambda i: (0, pair)),
            pl.BlockSpec((rows, 2 * LANES), lambda i: (0, pair)),
            pl.BlockSpec((rows, 2 * LANES), lambda i: (0, pair)),
            ANY,
        ],
        out_specs=[whole(s) for s in outs],
        scratch_shapes=[
            pltpu.VMEM((2, rows, LANES), F32),
            pltpu.VMEM((2, rows, LANES), F32),
            pltpu.VMEM((2, LANES, GROUP), BF),
            pltpu.VMEM((2, GROUP, LANES), BF),
            pltpu.VMEM((2, rows, LANES), BF),
            pltpu.VMEM((2, block, GROUP), F32),
        ],
        compiler_params=limit(28),
        cost_estimate=AHEAD,
    )(offsets, q, own, theirs, after)


def pair_columns(pair):
    return (
        slice(pair * LANES, (pair + 1) * LANES),
        slice(2 * pair * LANES, (2 * pair + 1) * LANES),
        slice((2 * pair + 1) * LANES, (2 * pair + 2) * LANES),
    )


def blend(old, old_peak, more, more_peak):
    top = jnp.maximum(old_peak, more_peak)
    return old * jnp.exp2(old_peak - top) + more * jnp.exp2(more_peak - top), top


def fetch(pieces, landed, sems):
    started, at = [], 0
    for i, piece in enumerate(pieces):
        rows = piece.shape[0]
        copy = pltpu.make_async_copy(piece, landed.at[pl.ds(at, rows), :], sems.at[i])
        copy.start()
        started.append((at, rows, copy))
        at += rows
    return started


def fill_pieces(started, landed, keys, values):
    for at, rows, copy in started:
        copy.wait()
        for pair in range(2):
            _, k_at, v_at = pair_columns(pair)
            fill(
                keys.at[pair],
                values.at[pair],
                at,
                landed[at : at + rows, k_at],
                landed[at : at + rows, v_at],
            )


def middle_kernel(q, *refs, count):
    pieces, near_acc, near_peak = refs[:count], refs[count : count + 2], refs[count + 2 : count + 4]
    acc_out, peak_out, keys, values, slots, landed, sems = refs[count + 4 :]
    fill_pieces(fetch(pieces, landed, sems), landed, keys, values)
    rows = q.shape[0]
    jobs = []
    for pair in range(2):
        lanes = pair_columns(pair)[0]
        for head in range(2):

            def done(acc, peak, pair=pair, head=head):
                new, top = blend(near_acc[pair][head], near_peak[pair][head], acc, peak)
                acc_out[2 * pair + head] = new
                peak_out[2 * pair + head] = top

            jobs.append(
                (
                    lambda lanes=lanes, head=head: split_queries(q[:, lanes], head),
                    keys[pair, head],
                    values[pair, head],
                    done,
                    rows,
                )
            )
    attend(jobs, slots)


def middle_attention(q, pieces, near_acc, near_peak):
    rows, own = q.shape
    heads = own // HEAD_DIM
    return pl.pallas_call(
        functools.partial(middle_kernel, count=len(pieces)),
        out_shape=[shape(heads, rows, LANES, dtype=F32)] * 2,
        in_specs=[VMEM] + [ANY] * len(pieces) + [VMEM] * 4,
        out_specs=[VMEM] * 2,
        scratch_shapes=[
            pltpu.VMEM((2, 2, LANES, GROUP), BF),
            pltpu.VMEM((2, 2, GROUP, LANES), BF),
            pltpu.VMEM((2, rows, GROUP), F32),
            pltpu.VMEM((GROUP, 2 * own), BF),
            pltpu.SemaphoreType.DMA((len(pieces),)),
        ],
        compiler_params=limit(24),
        cost_estimate=AHEAD,
    )(q, *pieces, *near_acc, *near_peak)


def far_kernel(offsets, qf, *refs, count):
    pieces, (near_acc, near_peak) = refs[:count], (refs[count : count + 2], refs[count + 2 : count + 4])
    mid_acc, mid_peak, out, keys, values, slots, acc, peak, far_rows, far_total, landed, sems = refs[
        count + 4 :
    ]
    started = fetch(pieces, landed, sems)
    mid, few = mid_acc.shape[1], qf.shape[0]
    acc[...] = mid_acc[...]
    peak[...] = mid_peak[...]
    fill_pieces(started, landed, keys, values)
    jobs = []
    for pair in range(2):
        lanes = pair_columns(pair)[0]
        for head in range(2):

            def done(more, more_peak, pair=pair, head=head):
                index = 2 * pair + head
                o_mid, o_far = offset_of(offsets, index, 0), offset_of(offsets, index, 1)
                shared = lax.rem(o_far, MID_RATE) == o_mid
                chosen = pl.ds(
                    lax.div(o_far, MID_RATE), few, stride=FAR_RATE // MID_RATE
                )
                held, held_peak = acc.at[index][chosen, :], peak.at[index][chosen, :]
                old = jnp.where(shared, held, near_acc[pair][head])
                old_peak = jnp.where(shared, held_peak, near_peak[pair][head])
                new, top = blend(old, old_peak, more, more_peak)
                acc.at[index][chosen, :] = jnp.where(shared, new, held)
                far_rows[index] = jnp.where(shared, 0.0, new)
                far_total[index] = jnp.where(shared, 1.0, new)

            jobs.append(
                (
                    lambda lanes=lanes, head=head: split_queries(qf[:, lanes], head),
                    keys[pair, head],
                    values[pair, head],
                    done,
                    few,
                )
            )
    attend(jobs, slots)
    for pair in range(2):
        lanes = pair_columns(pair)[0]
        out[:mid, lanes] = normalised(acc[2 * pair], acc[2 * pair + 1])
        out[mid : mid + few, lanes] = normalised(
            far_rows[2 * pair], far_rows[2 * pair + 1], far_total[2 * pair], far_total[2 * pair + 1]
        )
    row = lax.broadcasted_iota(jnp.int32, (NOTES, out.shape[1]), 0)
    told = jnp.zeros(row.shape, F32)
    for head in range(offsets.shape[1]):
        for which in range(2):
            value = offset_of(offsets, head, which).astype(F32)
            told = jnp.where(row == 2 * head + which, value, told)
    out[mid + few :, :] = told.astype(BF)


def far_attention(offsets, qf, pieces, near_acc, near_peak, mid_acc, mid_peak):
    few, own = qf.shape
    heads, mid = mid_acc.shape[:2]
    return pl.pallas_call(
        functools.partial(far_kernel, count=len(pieces)),
        out_shape=shape(mid + few + NOTES, own),
        in_specs=[VMEM] * 2 + [ANY] * len(pieces) + [VMEM] * 6,
        out_specs=VMEM,
        scratch_shapes=[
            pltpu.VMEM((2, 2, LANES, GROUP), BF),
            pltpu.VMEM((2, 2, GROUP, LANES), BF),
            pltpu.VMEM((2, few, GROUP), F32),
            pltpu.VMEM((heads, mid, LANES), F32),
            pltpu.VMEM((heads, mid, LANES), F32),
            pltpu.VMEM((heads, few, LANES), F32),
            pltpu.VMEM((heads, few, LANES), F32),
            pltpu.VMEM((GROUP, 2 * own), BF),
            pltpu.SemaphoreType.DMA((len(pieces),)),
        ],
        compiler_params=limit(20),
    )(offsets, qf, *pieces, *near_acc, *near_peak, mid_acc, mid_peak)


def told_offset(notes, pair, head, which):
    index = 2 * (2 * pair + head) + which
    return jnp.max(notes[index : index + 1, :]).astype(jnp.int32)


def weight_rows(me, d, pair, width):
    step = (0, 3, 1, 2)[d]
    first = lax.rem(me[0] + step, 4) * width + pair * LANES
    return pl.ds(pl.multiple_of(first, LANES), LANES)


def late_kernel(me, own, back, ahead, across, weight, out, w_out, told, sem):
    rows, width = out.shape[1], 2 * LANES
    left = left_lanes()
    mid = rows // MID_RATE
    noted = mid + rows // FAR_RATE
    columns = pl.ds(pl.multiple_of(me[0] * width, width), width)
    copy = pltpu.make_async_copy(weight.at[:, columns], w_out, sem)
    copy.start()
    for side in range(2):
        out[side] = jnp.zeros((rows, LANES), F32)
    copy.wait()
    for d, source in enumerate((own, back, ahead, across)):
        told[d] = source[noted : noted + NOTES, :LANES]
        notes = told[d].astype(F32)
        for pair in range(2):
            late = source[:, pair * LANES : (pair + 1) * LANES]
            zero = jnp.zeros_like(late)
            rows_of = w_out[weight_rows(me, d, pair, width), :]
            for head in range(2):
                part = jnp.where(left, late, zero) if head == 0 else jnp.where(left, zero, late)
                term = jnp.dot(part, rows_of, preferred_element_type=F32)
                for which, at, rate in ((0, 0, MID_RATE), (1, mid, FAR_RATE)):
                    count = rows // rate
                    chosen = pl.ds(told_offset(notes, pair, head, which), count, stride=rate)
                    for side in range(2):
                        target = out.at[side]
                        lanes = slice(side * LANES, (side + 1) * LANES)
                        target[chosen, :] = target[chosen, :] + term[at : at + count, lanes]


def late_product(me, lates, weight, rows):
    depth, own = weight.shape[0], lates[0].shape[1]
    return pl.pallas_call(
        late_kernel,
        out_shape=[shape(2, rows, LANES, dtype=F32), shape(depth, own), shape(4, NOTES, LANES)],
        in_specs=[SMEM] + [VMEM] * 4 + [ANY],
        out_specs=[VMEM] * 3,
        scratch_shapes=[pltpu.SemaphoreType.DMA],
        compiler_params=limit(16),
    )(me, *lates, weight)


def final_kernel(me, late, w, told, *refs, plan, count):
    arrays, (out, rows32) = refs[:count], refs[count:]
    rows, width = out.shape
    left = left_lanes()
    for slot, parts in enumerate(plan):
        d, pair = slot // 2, slot % 2
        target = rows32.at[slot]
        notes = told[d].astype(F32)
        at = 0
        for index, first, length in parts:
            target[at : at + length, :] = arrays[index][first : first + length, :].astype(F32)
            at += length
        for which, rate in ((0, MID_RATE), (1, FAR_RATE)):
            for head in range(2):
                chosen = pl.ds(told_offset(notes, pair, head, which), rows // rate, stride=rate)
                old = target[chosen, :]
                target[chosen, :] = jnp.where(left, 0.0, old) if head == 0 else jnp.where(left, old, 0.0)
    block = 256
    for r in range(rows // block):
        at = slice(r * block, (r + 1) * block)
        total = jnp.concatenate([late[0, at, :], late[1, at, :]], axis=1)
        for d in range(4):
            first = weight_rows(me, d, 0, width).start
            rows_of = w[pl.ds(pl.multiple_of(first, width), width), :]
            part = jnp.concatenate([rows32[2 * d, at, :], rows32[2 * d + 1, at, :]], axis=1).astype(BF)
            total = total + jnp.dot(part, rows_of, preferred_element_type=F32)
        out[at, :] = total.astype(BF)


def final_product(me, late, w, told, pieces):
    arrays, plan = [], []
    for parts in pieces:
        entry = []
        for array, first, length in parts:
            known = [i for i, a in enumerate(arrays) if a is array]
            if not known:
                arrays.append(array)
            entry.append((known[0] if known else len(arrays) - 1, first, length))
        plan.append(tuple(entry))
    rows, own = late.shape[1], w.shape[1]
    return pl.pallas_call(
        functools.partial(final_kernel, plan=tuple(plan), count=len(arrays)),
        out_shape=shape(rows, own),
        in_specs=[SMEM] + [VMEM] * (3 + len(arrays)),
        out_specs=VMEM,
        scratch_shapes=[pltpu.VMEM((8, rows, LANES), F32)],
        compiler_params=limit(24),
    )(me, late, w, told, *arrays)


def seg_move(array, target):
    pairs = []
    for i in range(64):
        x, z, core = i // 16, i // 2 % 8, i % 2
        x, z, core = target(x, z, core)
        pairs.append((i, (x % 4 * 8 + z % 8) * 2 + core))
    return lax.ppermute(array, "seg", pairs)


def swap_core(array):
    return seg_move(array, lambda x, z, core: (x, z, 1 - core))


def near_z(array, distance):
    return seg_move(array, lambda x, z, core: (x, z ^ distance, core))


def in_line(array):
    return seg_move(
        array, lambda x, z, core: (x, z // 4 * 4 + (z + (1 if core == 0 else 3)) % 4, core)
    )


def both_ways(array, distance):
    return seg_move(array, lambda x, z, core: (x, z + (distance if core == 0 else -distance), core))


def along_x(array, distance):
    return seg_move(array, lambda x, z, core: (x ^ distance, z, core))


def shift_head(array, distance):
    return lax.ppermute(array, "head", [(i, (i + distance) % 4) for i in range(4)])


def assemble_kernel(*refs, plan, count):
    arrays, outs = refs[:count], refs[-len(plan) :]
    for out, parts in zip(outs, plan):
        at = 0
        for index, first, rows in parts:
            out[at : at + rows, :] = arrays[index][first : first + rows, :]
            at += rows


def assemble(wanted, after=None):
    arrays, plan = [], []
    for parts in wanted:
        entry = []
        for array, first, rows in parts:
            entry.append((len(arrays), first, rows))
            arrays.append(array)
        plan.append(tuple(entry))
    extra = [] if after is None else [after]
    return pl.pallas_call(
        functools.partial(assemble_kernel, plan=tuple(plan), count=len(arrays)),
        out_shape=[
            shape(sum(part[2] for part in parts), parts[0][0].shape[1]) for parts in wanted
        ],
        in_specs=[VMEM] * len(arrays) + [ANY] * len(extra),
        out_specs=[VMEM] * len(wanted),
        compiler_params=limit(8),
    )(*arrays, *extra)


def pass_kernel(*refs):
    del refs


def hold(arrays, after, **options):
    count = len(arrays)
    return pl.pallas_call(
        pass_kernel,
        out_shape=[shape(*a.shape, dtype=a.dtype) for a in arrays],
        in_specs=[ANY] * (count + 1),
        out_specs=[ANY] * count,
        input_output_aliases={i: i for i in range(count)},
        compiler_params=limit(2),
        **options,
    )(*arrays, after)


def fence(arrays, after):
    return hold(arrays, after, cost_estimate=AHEAD)


def shards(tokens, norm_gain, qkv_weight, out_weight, offsets):
    me = lax.axis_index("head").astype(jnp.int32).reshape(1)
    offsets = offsets.T
    q, kv, qm, kvm, qf, kvf = project(offsets, tokens, norm_gain, qkv_weight)
    few, some = kvf.shape[0], kvm.shape[0]
    (chip,) = assemble([[(kvf, 0, few), (swap_core(kvf), 0, few)]])
    one, two = both_ways(chip, 1), both_ways(chip, 2)
    kv, kvm = hold([kv, kvm], chip)
    other = swap_core(kv)
    kvm_other = swap_core(kvm)
    (onward,) = assemble([[(chip, 0, 2 * few), (one, 0, few)]])
    three = both_ways(onward, 3)
    (middle_chip,) = assemble([[(kvm, 0, some), (kvm_other, 0, some)]], onward)
    beside = in_line(middle_chip)
    early0, *near0 = near_attention(offsets, q, 0, kv, other, middle_chip)
    (line,) = assemble(
        [[(kvf, 0, few), (one, 0, 2 * few), (two, 0, 2 * few), (three, 0, 3 * few)]], early0
    )
    columns = [along_x(line, distance) for distance in (1, 2, 3)]
    early1, *near1 = near_attention(offsets, q, 1, kv, other, line)
    (own_half,) = assemble([[(beside, 0, some)]], early1)
    across = in_line(own_half)
    rows = early1.shape[0]
    half = rows // 2
    (early,) = assemble([[(early0, 0, rows), (early1, 0, rows)]])
    back, ahead = shift_head(early, 1), shift_head(early, -1)
    (far_gathered,) = assemble([[(piece, 0, 8 * few) for piece in (line, *columns)]], early)
    (gathered,) = assemble([[(beside, 0, 2 * some), (across, 0, some)]], far_gathered)
    middles = [kvm, kvm_other, gathered, swap_core(gathered)]
    fars = [far_gathered, swap_core(far_gathered)]
    mid_acc, mid_peak = middle_attention(qm, middles, (near0[0], near1[0]), (near0[1], near1[1]))
    late = far_attention(
        offsets, qf, fars, (near0[2], near1[2]), (near0[3], near1[3]), mid_acc, mid_peak
    )
    lates = [late] + [shift_head(late, d) for d in (1, -1, 2)]
    top, bottom = assemble(
        [[(back, 0, half), (back, rows, half)], [(ahead, half, half), (ahead, rows + half, half)]],
        late,
    )
    top, bottom = shift_head(top, 1), shift_head(bottom, -1)
    late_sum, w, told = late_product(me, lates, out_weight, rows)
    return final_product(
        me,
        late_sum,
        w,
        told,
        [
            [(early, 0, rows)],
            [(early, rows, rows)],
            [(back, 0, rows)],
            [(back, rows, rows)],
            [(ahead, 0, rows)],
            [(ahead, rows, rows)],
            [(top, 0, half), (bottom, 0, half)],
            [(top, half, half), (bottom, half, half)],
        ],
    )


def solution(mesh):
    placed = (P("seg", None), P(), P(None, None, "head"), P(), P("head", None))
    return jax.shard_map(
        shards, mesh=mesh, in_specs=placed, out_specs=P("seg", "head"), check_vma=False
    )
```
